128 devices in a mesh: grp: 4 (over y), blk: 32 (over x, z, core).
Axes of the slice: x: 4, y: 4, z: 4, core: 2. Of those that a mesh axis runs over, the one named last changes fastest.
Arguments:
- tiles: float32 [4096, 8, 128, 128], P(('grp', 'blk')), may hold values from -0.5 to 0.5
- coeffs: float32 [32768, 128], P('blk'), may hold values from -0.25 to 0.25
- domains: int32 [256, 128], P('blk'), may hold values 0 or 1
- tile_owner: int32 [4096, 1], P(('grp', 'blk')), may hold values from 0 to 31; in each aligned block of 32 rows (0 to 31, 32 to 63, ...) at most 2 rows name the same one
- tile_local: int32 [4096], P(('grp', 'blk')), may hold values from 0 to 7
- tile_aux: int32 [4096], P(('grp', 'blk')), may hold values from 0 to 3
- pair_owner: int32 [1152, 1], P('blk'), may hold values from 0 to 31; in each aligned block of 36 rows (0 to 35, 36 to 71, ...) at most 2 rows name the same one
Outputs:
- owned: float32 [2048, 128, 128], P('blk')
The draws below stay inside these ranges and needn't reach their ends.
Inputs may be any that keep to these rules, and one draw needn't show every extreme that they name: `tile_owner`: in the rows of one device (aligned blocks of 32) no owner is named more than 2 times, a bound that some block reaches. `pair_owner`: in the rows of one device (aligned blocks of 36) no owner is named more than 2 times, a bound that some block reaches.
All inputs are finite; a program needn't handle non-finite values. No bound on the sum of `domains` on one device may be relied on, other than what follows from the above.
Results may differ from the reference program's by a relative error of at most 0.0003.
Values sent between devices are 32-bit elements; how exact they have to be, the bound alone decides.
A program may use at most 128 MiB of HBM per device.

```python
import math
import jax
import jax.numpy as jnp
import numpy as np
from jax import lax

ROWB = 128
NOCC = 128
AB = 8
AUXG = 32
MB = 8
TPM = 4
NA = 4
TD = 32
PD = 36
RQ = 2
CAP = 2
NBALL = 256
N_GRP = 4
N_BLK = 32
DEVICES = 128


def with_ends(array, key, least, top_value):
    place = [jax.random.randint(jax.random.fold_in(key, axis), (), 0, length) for axis, length in enumerate(array.shape)]
    main_axis = array.shape.index(max(array.shape))
    neighbour = place[:main_axis] + [(place[main_axis] + 1) % array.shape[main_axis]] + place[main_axis + 1:]
    return array.at[tuple(place)].set(least).at[tuple(neighbour)].set(top_value)


def shard_levels(stream_key, shape, split, low, largest):
    def one(axis_at, parts):
        draws = jax.random.uniform(jax.random.fold_in(jax.random.fold_in(stream_key, 6), axis_at), (parts,), jnp.float32, low / len(split), largest / len(split))
        return jnp.repeat(jnp.exp(draws), shape[axis_at] // parts).reshape((-1,) + (1,) * (len(shape) - axis_at - 1))

    gain = one(*split[0])
    for cut in split[1:]:
        gain = gain * one(*cut)
    return gain


def routed_block(own_key, own, number, rows, number_of, top, bound, skew):
    order = jax.random.permutation(own_key, number_of)
    crowded, usual = portions_of(number_of, rows * top, bound, skew, True), portions_of(number_of, rows * top, bound, skew, False)
    places = jnp.arange(number_of)

    def named(tallies, turn):
        used = int((tallies > 0).sum())
        fixed = max(1, used // 4)
        shifted = fixed + (places - fixed + turn * (used - fixed)) % max(1, number_of - fixed)
        return jnp.zeros((number_of,), jnp.int32).at[order[jnp.where(places < fixed, places, shifted)]].set(jnp.asarray(tallies, jnp.int32))

    tallies = jnp.where(number % 4 == 0, named(crowded, number // 4), named(usual, number - number // 4 - 1))
    mixed = jax.random.permutation(jax.random.fold_in(own, 3), number_of)
    donor, sink = mixed[0:number_of // 2 * 2:2], mixed[1:number_of // 2 * 2:2]
    slack = jnp.minimum(tallies[donor] - 1, bound - tallies[sink]) // 2
    slack = jnp.where((donor == order[0]) | (sink == order[0]) | (tallies[sink] == 0), 0, jnp.maximum(slack, 0))
    shifted = jax.random.randint(jax.random.fold_in(own, 4), (number_of // 2,), 0, 1 << 20) % (slack + 1)
    tallies = tallies.at[donor].add(-shifted).at[sink].add(shifted)
    items = jnp.searchsorted(jnp.cumsum(tallies), jnp.arange(rows * top), side="right").astype(jnp.int32)
    grid = items.reshape(top, rows).T
    grid = grid[jax.random.permutation(jax.random.fold_in(own, 1), rows)]
    turn = jax.random.randint(jax.random.fold_in(own, 2), (rows, 1), 0, top)
    return jnp.take_along_axis(grid, (jnp.arange(top)[None, :] + turn) % top, axis=1)


def portions_of(amount, total, most, slope, full):
    loads = [(1 << 20) // math.isqrt(standing ** slope) + 1 for standing in range(1, amount + 1)]
    largest = most if full else min(most, max(-(-total // amount), total * loads[0] // sum(loads)))
    least = 1 if total - largest >= amount - 1 else 0
    holding, spare = [largest] + [least] * (amount - 1), total - largest - least * (amount - 1)
    while spare > 0:
        candidates = [i for i in range(1, amount) if holding[i] < largest] or [i for i in range(1, amount) if holding[i] < most]
        pool, budget = sum([loads[i] for i in candidates]), spare
        for i in candidates:
            extra = min(most - holding[i], max(1, budget * loads[i] // pool), spare)
            holding[i] = holding[i] + extra
            spare = spare - extra
    return np.array(holding)


def scatter_about(key, extent, width, limit, split=(), dtype=jnp.bfloat16):
    entries = width * jax.random.normal(key, extent, jnp.float32)
    if split:
        entries = entries * shard_levels(key, extent, split, -0.22, 0.18)
    return jnp.clip(entries, -limit, limit).astype(dtype)


def setup_inputs(seed: int = 0) -> dict:
    streams_of = jax.random.split(jax.random.key(seed), 8)
    tiles = scatter_about(streams_of[0], (DEVICES * TD, AB, ROWB, ROWB), ROWB ** -0.5, 0.5, ((0, 128),), jnp.float32)
    coeffs = scatter_about(streams_of[1], (NBALL * ROWB, NOCC), (AUXG * NOCC // 8) ** -0.5, 0.25, ((0, 32),), jnp.float32)
    domains = with_ends((jax.random.randint(streams_of[2], (NBALL, NOCC), 0, 2) < 1).astype(jnp.int32), jax.random.fold_in(streams_of[2], 1), 0, 1)
    tile_owner_keys = jax.random.split(jax.random.fold_in(streams_of[3], 1), (DEVICES * TD) // TD)
    tile_owner_turns = jax.random.permutation(jax.random.fold_in(streams_of[3], 3), (DEVICES * TD) // TD)
    tile_owner = jax.vmap(lambda own, number: routed_block(jax.random.fold_in(streams_of[3], 2), own, number, TD, N_BLK, 1, RQ, 2))(tile_owner_keys, tile_owner_turns).reshape((DEVICES * TD, 1))
    tile_local = with_ends(jax.random.randint(streams_of[4], (DEVICES * TD,), 0, MB), jax.random.fold_in(streams_of[4], 1), 0, MB - 1).astype(jnp.int32)
    tile_aux = with_ends(jax.random.randint(streams_of[5], (DEVICES * TD,), 0, NA), jax.random.fold_in(streams_of[5], 1), 0, NA - 1).astype(jnp.int32)
    pair_owner_keys = jax.random.split(jax.random.fold_in(streams_of[6], 1), (N_BLK * PD) // PD)
    pair_owner_turns = jax.random.permutation(jax.random.fold_in(streams_of[6], 3), (N_BLK * PD) // PD)
    pair_owner = jax.vmap(lambda own, number: routed_block(jax.random.fold_in(streams_of[6], 2), own, number, PD, N_BLK, 1, CAP, 2))(pair_owner_keys, pair_owner_turns).reshape((N_BLK * PD, 1))
    return {"tiles": tiles, "coeffs": coeffs, "domains": domains, "tile_owner": tile_owner, "tile_local": tile_local, "tile_aux": tile_aux, "pair_owner": pair_owner}


HIGH = lax.Precision.HIGHEST


def pair_rank(owner):
    count = owner.shape[0]
    index = jnp.arange(count).astype(jnp.int32)
    same = (owner[:, None] == owner[None, :]) & (index[None, :] < index[:, None])
    return jnp.sum(same.astype(jnp.int32), axis=1).astype(jnp.int32)


def build_factors(tile_group, picked, aux_index, domain_rows):
    products = jnp.einsum("eprs,esj->eprj", tile_group, picked, precision=HIGH)
    local_block = (jnp.arange(TD) // TPM).astype(jnp.int32)
    which = (local_block * NA + aux_index).astype(jnp.int32)
    onehot = (which[:, None] == jnp.arange(MB * NA).astype(jnp.int32)[None, :]).astype(jnp.float32)
    factors = jnp.einsum("ek,eprj->kprj", onehot, products, precision=HIGH)
    factors = factors.reshape(MB, AUXG, ROWB, NOCC)
    return factors * domain_rows.astype(jnp.float32)[:, None, None, :]


def reference(tiles, coeffs, domains, tile_owner, tile_local, tile_aux, pair_owner):
    tile_grid = tiles.reshape(N_GRP, N_BLK, TD, AB, ROWB, ROWB)
    owner_grid = tile_owner.reshape(N_GRP, N_BLK, TD)
    local_grid = tile_local.reshape(N_GRP, N_BLK, TD)
    aux_grid = tile_aux.reshape(N_GRP, N_BLK, TD)
    coeff_blocks = coeffs.reshape(NBALL, ROWB, NOCC)
    domain_grid = domains.reshape(N_BLK, MB, NOCC)
    pair_grid = pair_owner.reshape(N_BLK, PD)
    first_np, second_np = np.triu_indices(MB)
    first = jnp.asarray(first_np.astype(np.int32))
    second = jnp.asarray(second_np.astype(np.int32))

    def one_device(device):
        pieces = []
        for group in range(N_GRP):
            source = (owner_grid[group, device] * MB + local_grid[group, device]).astype(jnp.int32)
            picked = coeff_blocks[source]
            pieces.append(build_factors(tile_grid[group, device], picked, aux_grid[group, device], domain_grid[device]))
        factors = jnp.concatenate(pieces, axis=1)
        flat = jnp.transpose(factors, (0, 2, 1, 3)).reshape(MB, ROWB, N_GRP * AUXG * NOCC)
        gram = jnp.einsum("arx,bsx->abrs", flat, flat, precision=HIGH)
        partial_value = gram[first, second]
        owner = pair_grid[device]
        slot = (owner * CAP + pair_rank(owner)).astype(jnp.int32)
        onehot = (jnp.arange(N_BLK * CAP).astype(jnp.int32)[:, None] == slot[None, :]).astype(jnp.float32)
        return jnp.einsum("kq,qrs->krs", onehot, partial_value, precision=HIGH)

    sent = lax.map(one_device, jnp.arange(N_BLK).astype(jnp.int32))
    sent = sent.reshape(N_BLK, N_BLK, CAP, ROWB, ROWB)
    return jnp.transpose(sent, (1, 0, 2, 3, 4)).reshape(N_BLK * N_BLK * CAP, ROWB, ROWB)
```

```python
import functools
import jax, jax.numpy as jnp
import numpy as np
from jax import lax
from jax.experimental import pallas as pl
from jax.experimental.pallas import tpu as pltpu
from jax.sharding import PartitionSpec as P

F32, BF16 = jnp.float32, jnp.bfloat16
NT = (((1,), (1,)), ((), ()))

def split(v):
    hi = v.astype(BF16)
    return hi, (v - hi.astype(F32)).astype(BF16)

def k2_body(src, aux, t, c0, c1, c2, c3, dom, out, F, H, L):
    m = pl.program_id(0)
    F[...] = jnp.zeros_like(F)
    for j, c in enumerate((c0, c1, c2, c3)):
        a = aux[m * 4 + j]
        ch, cl = split(c[0])
        w = jnp.concatenate([ch, cl], axis=1)
        w = jnp.concatenate([w, w], axis=0)
        for q in range(8):
            th, tl = split(t[j, q])
            p = jnp.dot(jnp.concatenate([th, tl], axis=1), w, preferred_element_type=F32)
            F[a, q] += p[:, :128] + p[:, 128:]
    mask = dom[0].astype(F32)
    rows = pl.ds(m * 128, 128)
    for a in range(4):
        for q in range(8):
            hi, lo = split(F[a, q] * mask)
            cols = pl.ds((a * 8 + q) * 128, 128)
            H[rows, cols] = hi
            L[rows, cols] = lo

    @pl.when(m == 7)
    def _():
        gram(out, H, L)

def gram(out, H, L):
    for J in range(4):
        @pl.loop(0, J + 1)
        def _(I):
            ri = pl.ds(I * 256, 256)
            rj = pl.ds(J * 256, 256)
            g = lax.dot_general(H[ri, :], H[rj, :], NT, preferred_element_type=F32)
            g += lax.dot_general(L[ri, :], H[rj, :], NT, preferred_element_type=F32)
            g += lax.dot_general(H[ri, :], L[rj, :], NT, preferred_element_type=F32)
            for x in range(2):
                mm = 2 * I + x
                base = mm * 8 - mm * (mm - 1) // 2 - mm
                for y in range(2):
                    nn = 2 * J + y
                    blk = g[x * 128:(x + 1) * 128, y * 128:(y + 1) * 128]
                    if x == 1 and y == 0:
                        @pl.when(I < J)
                        def _():
                            out[base + nn] = blk
                    else:
                        out[base + nn] = blk

def k2(tiles, coeffs, domains, source, aux):
    cs = [pl.BlockSpec((1, 128, 128), functools.partial(lambda j, m, s, a: (s[m * 4 + j], 0, 0), j)) for j in range(4)]
    return pl.pallas_call(
        k2_body,
        grid_spec=pltpu.PrefetchScalarGridSpec(
            num_scalar_prefetch=2, grid=(8,),
            in_specs=[pl.BlockSpec((4, 8, 128, 128), lambda m, s, a: (m, 0, 0, 0))] + cs +
                     [pl.BlockSpec((1, 1, 128), lambda m, s, a: (m, 0, 0))],
            out_specs=pl.BlockSpec((36, 128, 128), lambda m, s, a: (0, 0, 0)),
            scratch_shapes=[pltpu.VMEM((4, 8, 128, 128), F32), pltpu.VMEM((1024, 4096), BF16), pltpu.VMEM((1024, 4096), BF16)]),
        out_shape=jax.ShapeDtypeStruct((36, 128, 128), F32),
        compiler_params=pltpu.CompilerParams(vmem_limit_bytes=60 * 2**20),
        cost_estimate=pl.CostEstimate(flops=2 * 10**10, bytes_accessed=22 * 10**6, transcendentals=0),
    )(source, aux, tiles, coeffs, coeffs, coeffs, coeffs, domains)


def pair_rank(owner):
    index = jnp.arange(owner.shape[0])
    same = (owner[:, None] == owner[None, :]) & (index[None, :] < index[:, None])
    return jnp.sum(same.astype(jnp.int32), axis=1)


def on_device(tiles, coeffs, domains, tile_owner, tile_local, tile_aux, pair_owner):
    gathered = lax.all_gather(coeffs, "blk", axis=0, tiled=True).reshape(256, 128, 128)
    source = tile_owner[:, 0] * 8 + tile_local
    partial = k2(tiles, gathered, domains[:, None, :], source, tile_aux)
    targets = pair_owner[:, 0]
    slot = targets * 2 + pair_rank(targets)
    placing = (jnp.arange(64)[:, None] == slot[None, :]).astype(jnp.int32)
    used = jnp.sum(placing, axis=1)
    pair = jnp.sum(placing * jnp.arange(36)[None, :], axis=1)
    mine = lax.psum_scatter(partial, "grp", scatter_dimension=1, tiled=True)
    outgoing = jnp.where(used[:, None, None] > 0, mine[pair], 0.0)
    received = lax.all_to_all(outgoing, "blk", split_axis=0, concat_axis=0, tiled=True)
    return lax.all_gather(received, "grp", axis=1, tiled=True)


def solution(mesh):
    placed = (
        P(("grp", "blk"), None, None, None),
        P("blk", None),
        P("blk", None),
        P(("grp", "blk"), None),
        P(("grp", "blk")),
        P(("grp", "blk")),
        P("blk", None),
    )
    return jax.shard_map(
        on_device, mesh=mesh, in_specs=placed, out_specs=P("blk", None, None), check_vma=False
    )
```

```python
import functools
import jax, jax.numpy as jnp
from jax import lax
from jax.experimental import pallas as pl
from jax.experimental.pallas import tpu as pltpu
from jax.sharding import PartitionSpec as P

F32, BF16 = jnp.float32, jnp.bfloat16
NT = (((1,), (1,)), ((), ()))

MESH = pl.DeviceIdType.MESH


def split(v):
    hi = v.astype(BF16)
    return hi, (v - hi.astype(F32)).astype(BF16)

def k2_body(src, aux, t, c0, c1, c2, c3, dom, out, F, H, L):
    m = pl.program_id(0)
    F[...] = jnp.zeros_like(F)
    for j, c in enumerate((c0, c1, c2, c3)):
        a = aux[m * 4 + j]
        ch, cl = split(c[0])
        w = jnp.concatenate([ch, cl], axis=1)
        w = jnp.concatenate([w, w], axis=0)
        for q in range(8):
            th, tl = split(t[j, q])
            p = jnp.dot(jnp.concatenate([th, tl], axis=1), w, preferred_element_type=F32)
            F[a, q] += p[:, :128] + p[:, 128:]
    mask = dom[0].astype(F32)
    rows = pl.ds(m * 128, 128)
    for a in range(4):
        for q in range(8):
            hi, lo = split(F[a, q] * mask)
            cols = pl.ds((a * 8 + q) * 128, 128)
            H[rows, cols] = hi
            L[rows, cols] = lo

    @pl.when(m == 7)
    def _():
        gram(out, H, L)

def gram(out, H, L):
    for J in range(4):
        @pl.loop(0, J + 1)
        def _(I):
            ri = pl.ds(I * 256, 256)
            rj = pl.ds(J * 256, 256)
            g = lax.dot_general(H[ri, :], H[rj, :], NT, preferred_element_type=F32)
            g += lax.dot_general(L[ri, :], H[rj, :], NT, preferred_element_type=F32)
            g += lax.dot_general(H[ri, :], L[rj, :], NT, preferred_element_type=F32)
            for x in range(2):
                mm = 2 * I + x
                base = mm * 8 - mm * (mm - 1) // 2 - mm
                for y in range(2):
                    nn = 2 * J + y
                    blk = g[x * 128:(x + 1) * 128, y * 128:(y + 1) * 128]
                    if x == 1 and y == 0:
                        @pl.when(I < J)
                        def _():
                            out[base + nn] = blk
                    else:
                        out[base + nn] = blk

def k2(tiles, coeffs, domains, source, aux):
    cs = [pl.BlockSpec((1, 128, 128), functools.partial(lambda j, m, s, a: (s[m * 4 + j], 0, 0), j)) for j in range(4)]
    return pl.pallas_call(
        k2_body,
        grid_spec=pltpu.PrefetchScalarGridSpec(
            num_scalar_prefetch=2, grid=(8,),
            in_specs=[pl.BlockSpec((4, 8, 128, 128), lambda m, s, a: (m, 0, 0, 0))] + cs +
                     [pl.BlockSpec((1, 1, 128), lambda m, s, a: (m, 0, 0))],
            out_specs=pl.BlockSpec((36, 128, 128), lambda m, s, a: (0, 0, 0)),
            scratch_shapes=[pltpu.VMEM((4, 8, 128, 128), F32), pltpu.VMEM((1024, 4096), BF16), pltpu.VMEM((1024, 4096), BF16)]),
        out_shape=jax.ShapeDtypeStruct((36, 128, 128), F32),
        compiler_params=pltpu.CompilerParams(vmem_limit_bytes=60 * 2**20),
        cost_estimate=pl.CostEstimate(flops=2 * 10**10, bytes_accessed=22 * 10**6, transcendentals=0),
    )(source, aux, tiles, coeffs, coeffs, coeffs, coeffs, domains)


def coords():
    b = lax.axis_index("blk")
    y = lax.axis_index("grp")
    return b // 8, y, lax.rem(b // 2, 4), lax.rem(b, 2)


def index(x, z, c):
    return (lax.rem(x + 8, 4) * 4 + lax.rem(z + 8, 4)) * 2 + c


def enter(partners):
    barrier = pltpu.get_barrier_semaphore()
    for g, b in partners:
        pl.semaphore_signal(barrier, inc=1, device_id={"grp": g, "blk": b}, device_id_type=MESH)
    pl.semaphore_wait(barrier, len(partners))


def gather_body(own, out, send, recv, sib_send, sib_recv, local_sem):
    x, y, z, c = coords()
    me = index(x, z, c)
    other = index(x, z, 1 - c)
    axes = [((1, 0), (0, 1)), ((0, 1), (1, 0))]

    def at(part, du, dv):
        (ux, uz), (vx, vz) = axes[part]
        return index(x + du * ux + dv * vx, z + du * uz + dv * vz, c)

    enter([(y, index(x + 1, z, c)), (y, index(x - 1, z, c)), (y, index(x, z + 1, c)), (y, index(x, z - 1, c)), (y, other)])
    here = pltpu.make_async_copy(own, out.at[me], local_sem)
    here.start()
    sends, sibs = [], []
    count = [0, 0]

    def remote(src, dst, to, k):
        cp = pltpu.make_async_remote_copy(src_ref=src, dst_ref=dst, send_sem=send.at[k], recv_sem=recv.at[k],
                                          device_id={"grp": y, "blk": to}, device_id_type=MESH)
        return cp

    def sibling(src_dev, lo, n, src=None, other_dev=None):
        k = count[1]
        count[1] += 1
        ref = out.at[src_dev, pl.ds(lo, n)] if src is None else src
        cp = pltpu.make_async_remote_copy(src_ref=ref, dst_ref=out.at[src_dev, pl.ds(lo, n)], send_sem=sib_send.at[k],
                                          recv_sem=sib_recv.at[k], device_id={"grp": y, "blk": other}, device_id_type=MESH)
        cp.start()
        sibs.append((k, src_dev, lo, n, cp))

    table = {}

    def define(part, key, du, dv, lo, n):
        table[part, key] = (len(table), du, dv, part * 4 + lo, n)

    for part in range(2):
        define(part, "u+", -1, 0, 0, 4)
        define(part, "u-", 1, 0, 0, 4)
        define(part, "uu+", -2, 0, 0, 2)
        define(part, "uu-", 2, 0, 2, 2)
        for sign in (1, -1):
            for name, du, lo, n in (("0", 0, 0, 4), ("m", -1, 0, 4), ("p", 1, 0, 4), ("2l", 2, 0, 2), ("2h", 2, 2, 2)):
                define(part, ("v", sign, name), du, -sign, lo, n)
            for name, du in (("0", 0), ("m", -1), ("p", 1), ("2", 2)):
                define(part, ("vv", sign, name), du, -2 * sign, 0 if sign > 0 else 2, 2)

    def post(part, key, du_to, dv_to, src=None):
        k, du, dv, lo, n = table[part, key]
        source = at(part, du + du_to, dv + dv_to)
        region = out.at[source, pl.ds(lo, n)]
        cp = remote(region if src is None else src.at[pl.ds(lo, n)], region, at(part, du_to, dv_to), k)
        cp.start()
        sends.append(cp)

    def arrive(part, key, share=True):
        k, du, dv, lo, n = table[part, key]
        source = at(part, du, dv)
        region = out.at[source, pl.ds(lo, n)]
        remote(region, region, at(part, 0, 0), k).wait_recv()
        if share:
            sibling(source, lo, n)

    for part in range(2):
        post(part, "u+", 1, 0, own)
        post(part, "u-", -1, 0, own)
    for part in range(2):
        post(part, ("v", 1, "0"), 0, 1, own)
        post(part, ("v", -1, "0"), 0, -1, own)
    sibling(me, 0, 8, own)
    for key, name, fwd, step in (("u+", "m", "uu+", 1), ("u-", "p", "uu-", -1)):
        for part in range(2):
            arrive(part, key)
            post(part, fwd, step, 0)
            post(part, ("v", 1, name), 0, 1)
            post(part, ("v", -1, name), 0, -1)
    for sign in (1, -1):
        for part in range(2):
            arrive(part, ("v", sign, "0"))
            post(part, ("vv", sign, "0"), 0, sign)
    for key, name in (("uu+", "2l"), ("uu-", "2h")):
        for part in range(2):
            arrive(part, key)
            post(part, ("v", 1, name), 0, 1)
            post(part, ("v", -1, name), 0, -1)
    for name in ("m", "p"):
        for sign in (1, -1):
            for part in range(2):
                arrive(part, ("v", sign, name))
                post(part, ("vv", sign, name), 0, sign)
    for sign, name, drop in ((1, "2l", "2h"), (-1, "2h", "2l")):
        for part in range(2):
            arrive(part, ("v", sign, name))
            post(part, ("vv", sign, "2"), 0, sign)
            arrive(part, ("v", -sign, name))
    for name in ("0", "m", "p", "2"):
        for sign in (1, -1):
            for part in range(2):
                arrive(part, ("vv", sign, name))
    here.wait()
    for k, src_dev, lo, n, cp in sibs:
        theirs = src_dev + 1 - 2 * c
        region = out.at[theirs, pl.ds(lo, n)]
        pltpu.make_async_remote_copy(src_ref=region, dst_ref=region, send_sem=sib_send.at[k], recv_sem=sib_recv.at[k],
                                     device_id={"grp": y, "blk": other}, device_id_type=MESH).wait_recv()
        cp.wait_send()
    for cp in sends:
        cp.wait_send()


def gather(coeffs):
    return pl.pallas_call(
        gather_body,
        out_shape=jax.ShapeDtypeStruct((32, 8, 128, 128), F32),
        in_specs=[pl.BlockSpec(memory_space=pl.ANY)],
        out_specs=pl.BlockSpec(memory_space=pl.ANY),
        scratch_shapes=[pltpu.SemaphoreType.DMA((44,)), pltpu.SemaphoreType.DMA((44,)), pltpu.SemaphoreType.DMA((45,)),
                        pltpu.SemaphoreType.DMA((45,)), pltpu.SemaphoreType.DMA],
        compiler_params=pltpu.CompilerParams(collective_id=1, has_side_effects=True),
    )(coeffs.reshape(8, 128, 128))


def exchange_body(partial, pair, used, out, sums, placed, got, take, rs_send, rs_recv, a_send, a_recv, g_send, g_recv, local_sem):
    x, y, z, c = coords()
    me = index(x, z, c)

    def plane(d):
        return lax.rem(y + d + 4, 4)

    def peer(dx, d):
        return index(x + dx, z + d // 2, lax.rem(c + d, 2))

    barrier = pltpu.get_barrier_semaphore()
    for d in (1, 2, 3):
        pl.semaphore_signal(barrier, inc=1, device_id={"grp": plane(d), "blk": me}, device_id_type=MESH)

    @pl.loop(1, 32)
    def _(k):
        pl.semaphore_signal(barrier, inc=1, device_id={"grp": y, "blk": peer(k // 8, lax.rem(k, 8))}, device_id_type=MESH)

    pl.semaphore_wait(barrier, 34)

    rs = []
    for d in (1, 3, 2):
        cp = pltpu.make_async_remote_copy(
            src_ref=partial.at[:, pl.ds(32 * plane(d), 32), :], dst_ref=sums.at[d - 1], send_sem=rs_send.at[d - 1],
            recv_sem=rs_recv.at[d - 1], device_id={"grp": plane(d), "blk": me}, device_id_type=MESH)
        cp.start()
        rs.append(cp)
    for cp in rs:
        cp.wait_recv()

    @pl.loop(0, 36)
    def _(q):
        take[q] = (partial[q, pl.ds(32 * y, 32), :] + sums[0, q]) + (sums[1, q] + sums[2, q])

    @pl.loop(0, 64)
    def _(s):
        placed[s] = take[pair[s]] * used[s].astype(F32)

    def shipment(dx, d):
        to = peer(dx, d)
        return pltpu.make_async_remote_copy(
            src_ref=placed.at[pl.ds(2 * to, 2)], dst_ref=got.at[pl.ds(2 * me, 2)], send_sem=a_send.at[dx, d],
            recv_sem=a_recv.at[dx, d], device_id={"grp": y, "blk": to}, device_id_type=MESH)

    def arrival(dx, d):
        frm = index(x - dx, z - d // 2 + 4, lax.rem(c + d, 2))
        region = got.at[pl.ds(2 * frm, 2)]
        return pltpu.make_async_remote_copy(
            src_ref=region, dst_ref=region, send_sem=a_send.at[dx, d], recv_sem=a_recv.at[dx, d],
            device_id={"grp": y, "blk": me}, device_id_type=MESH)

    for dx in (0, 1, 3, 2):
        @pl.loop(1 if dx == 0 else 0, 8)
        def _(d):
            shipment(dx, d).start()
    mine = pltpu.make_async_copy(placed.at[pl.ds(2 * me, 2)], got.at[pl.ds(2 * me, 2)], local_sem.at[4])
    mine.start()
    mine.wait()

    def rows(plane_index):
        return pl.ds(32 * plane_index, 32)

    sends, locals_ = [], []
    for dx in (0, 1, 3, 2):
        @pl.loop(1 if dx == 0 else 0, 8)
        def _(d):
            arrival(dx, d).wait_recv()
        first = 16 * lax.rem(x - dx + 4, 4)
        for i, step in enumerate((1, -1)):
            cp = pltpu.make_async_remote_copy(
                src_ref=got.at[pl.ds(first, 16)], dst_ref=out.at[pl.ds(first, 16), rows(y)], send_sem=g_send.at[dx, i],
                recv_sem=g_recv.at[dx, i], device_id={"grp": plane(step), "blk": me}, device_id_type=MESH)
            cp.start()
            sends.append(cp)
        cp = pltpu.make_async_copy(got.at[pl.ds(first, 16)], out.at[pl.ds(first, 16), rows(y)], local_sem.at[dx])
        cp.start()
        locals_.append(cp)
    for dx in (0, 1, 3, 2):
        first = 16 * lax.rem(x - dx + 4, 4)
        for i, step in enumerate((1, -1)):
            region = out.at[pl.ds(first, 16), rows(plane(-step))]
            pltpu.make_async_remote_copy(
                src_ref=region, dst_ref=region, send_sem=g_send.at[dx, i], recv_sem=g_recv.at[dx, i],
                device_id={"grp": y, "blk": me}, device_id_type=MESH).wait_recv()
            half = out.at[pl.ds(first + 8 * i, 8), rows(plane(-step))]
            cp = pltpu.make_async_remote_copy(
                src_ref=half, dst_ref=half, send_sem=g_send.at[dx, 2 + i], recv_sem=g_recv.at[dx, 2 + i],
                device_id={"grp": plane(step), "blk": me}, device_id_type=MESH)
            cp.start()
            sends.append(cp)
    for dx in (0, 1, 3, 2):
        first = 16 * lax.rem(x - dx + 4, 4)
        for i in range(2):
            half = out.at[pl.ds(first + 8 * i, 8), rows(plane(2))]
            pltpu.make_async_remote_copy(
                src_ref=half, dst_ref=half, send_sem=g_send.at[dx, 2 + i], recv_sem=g_recv.at[dx, 2 + i],
                device_id={"grp": y, "blk": me}, device_id_type=MESH).wait_recv()
    for cp in locals_:
        cp.wait()
    for cp in rs + sends:
        cp.wait_send()
    for dx in range(4):
        @pl.loop(1 if dx == 0 else 0, 8)
        def _(d):
            shipment(dx, d).wait_send()


def exchange(partial, pair, used):
    vm = pl.BlockSpec(memory_space=pltpu.VMEM)
    sm = pl.BlockSpec(memory_space=pltpu.SMEM)
    dma = pltpu.SemaphoreType.DMA
    return pl.pallas_call(
        exchange_body,
        out_shape=jax.ShapeDtypeStruct((64, 128, 128), F32),
        in_specs=[vm, sm, sm],
        out_specs=pl.BlockSpec(memory_space=pl.ANY),
        scratch_shapes=[pltpu.VMEM((3, 36, 32, 128), F32), pltpu.VMEM((64, 32, 128), F32), pltpu.VMEM((64, 32, 128), F32),
                        pltpu.VMEM((36, 32, 128), F32),
                        dma((3,)), dma((3,)), dma((4, 8)), dma((4, 8)), dma((4, 4)), dma((4, 4)), dma((5,))],
        compiler_params=pltpu.CompilerParams(collective_id=2, has_side_effects=True, vmem_limit_bytes=32 * 2**20),
    )(partial, pair, used)


def pair_rank(owner):
    index = jnp.arange(owner.shape[0])
    same = (owner[:, None] == owner[None, :]) & (index[None, :] < index[:, None])
    return jnp.sum(same.astype(jnp.int32), axis=1)


def on_device(tiles, coeffs, domains, tile_owner, tile_local, tile_aux, pair_owner):
    gathered = gather(coeffs).reshape(256, 128, 128)
    source = tile_owner[:, 0] * 8 + tile_local
    partial = k2(tiles, gathered, domains[:, None, :], source, tile_aux)
    targets = pair_owner[:, 0]
    slot = targets * 2 + pair_rank(targets)
    placing = (jnp.arange(64)[:, None] == slot[None, :]).astype(jnp.int32)
    used = jnp.sum(placing, axis=1)
    pair = jnp.sum(placing * jnp.arange(36)[None, :], axis=1)
    return exchange(partial, pair, used)


def solution(mesh):
    placed = (
        P(("grp", "blk"), None, None, None),
        P("blk", None),
        P("blk", None),
        P(("grp", "blk"), None),
        P(("grp", "blk")),
        P(("grp", "blk")),
        P("blk", None),
    )
    return jax.shard_map(
        on_device, mesh=mesh, in_specs=placed, out_specs=P("blk", None, None), check_vma=False
    )
```

```python
import jax
import jax.numpy as jnp
import numpy as np
from jax import lax
from jax.experimental import pallas as pl
from jax.experimental.pallas import tpu as pltpu
from jax.sharding import PartitionSpec as P

F32, BF16 = jnp.float32, jnp.bfloat16
MESH = pl.DeviceIdType.MESH
NT = (((1,), (1,)), ((), ()))
CHUNKS = ((0, 8), (8, 7), (15, 8), (23, 6), (29, 7))


def places():
    spot = {}
    for m in range(4):
        for n in (6, 7):
            spot[m, n] = (n - 6) * 4 + m
        for n in (4, 5):
            spot[m, n] = 15 + (n - 4) * 4 + m
    for m in range(4, 8):
        for n in (6, 7):
            spot[m, n] = 8 + 3 * (n - 6) + m - 4
    for s, m in ((0, 4), (1, 0)):
        spot[m, m], spot[m, m + 1], spot[m + 1, m + 1] = 23 + 3 * s, 24 + 3 * s, 25 + 3 * s
    for m in range(4):
        for n in (2, 3):
            spot[m, n] = 29 + 3 * (n - 2) + m
    return np.array([spot[m, n] for m in range(8) for n in range(m, 8)], np.int32)


def split(v):
    hi = v.astype(BF16)
    return hi, (v - hi.astype(F32)).astype(BF16)


def coords():
    b = lax.axis_index("blk")
    return b // 8, lax.axis_index("grp"), lax.rem(b // 2, 4), lax.rem(b, 2)


def index(x, z, c):
    return (lax.rem(x + 8, 4) * 4 + lax.rem(z + 8, 4)) * 2 + c


def gather_coeffs(own, coef, sems, work):
    send, recv, sib_send, sib_recv, local_sem = sems
    x, y, z, c = coords()
    me = index(x, z, c)
    other = index(x, z, 1 - c)
    axes = [((1, 0), (0, 1)), ((0, 1), (1, 0))]

    def at(part, du, dv):
        (ux, uz), (vx, vz) = axes[part]
        return index(x + du * ux + dv * vx, z + du * uz + dv * vz, c)

    here = pltpu.make_async_copy(own, coef.at[me], local_sem)
    here.start()
    sends, sibs = [], []

    def remote(src, dst, to, s, r):
        return pltpu.make_async_remote_copy(src_ref=src, dst_ref=dst, send_sem=s, recv_sem=r,
                                            device_id={"grp": y, "blk": to}, device_id_type=MESH)

    def sibling(source, lo, n, src=None):
        k = len(sibs)
        region = coef.at[source, pl.ds(lo, n)]
        cp = remote(region if src is None else src, region, other, sib_send.at[k], sib_recv.at[k])
        cp.start()
        sibs.append((source, lo, n, cp))

    table = {}

    def define(part, key, du, dv, lo, n):
        table[part, key] = (len(table), du, dv, part * 4 + lo, n)

    for part in range(2):
        define(part, "u+", -1, 0, 0, 4)
        define(part, "u-", 1, 0, 0, 4)
        define(part, "uu+", -2, 0, 0, 2)
        define(part, "uu-", 2, 0, 2, 2)
        for sign in (1, -1):
            for name, du, lo, n in (("0", 0, 0, 4), ("m", -1, 0, 4), ("p", 1, 0, 4), ("2l", 2, 0, 2), ("2h", 2, 2, 2)):
                define(part, ("v", sign, name), du, -sign, lo, n)
            for name, du in (("0", 0), ("m", -1), ("p", 1), ("2", 2)):
                define(part, ("vv", sign, name), du, -2 * sign, 0 if sign > 0 else 2, 2)

    def post(part, key, du_to, dv_to, src=None):
        k, du, dv, lo, n = table[part, key]
        region = coef.at[at(part, du + du_to, dv + dv_to), pl.ds(lo, n)]
        cp = remote(region if src is None else src.at[pl.ds(lo, n)], region, at(part, du_to, dv_to), send.at[k], recv.at[k])
        cp.start()
        sends.append(cp)

    def arrive(part, key):
        k, du, dv, lo, n = table[part, key]
        source = at(part, du, dv)
        region = coef.at[source, pl.ds(lo, n)]
        remote(region, region, me, send.at[k], recv.at[k]).wait_recv()
        sibling(source, lo, n)

    def meanwhile():
        if work:
            work.pop(0)()

    for part in range(2):
        post(part, "u+", 1, 0, own)
        post(part, "u-", -1, 0, own)
    for part in range(2):
        post(part, ("v", 1, "0"), 0, 1, own)
        post(part, ("v", -1, "0"), 0, -1, own)
    sibling(me, 0, 8, own)
    meanwhile()
    meanwhile()
    for key, name, fwd, step in (("u+", "m", "uu+", 1), ("u-", "p", "uu-", -1)):
        for part in range(2):
            arrive(part, key)
            post(part, fwd, step, 0)
            post(part, ("v", 1, name), 0, 1)
            post(part, ("v", -1, name), 0, -1)
    meanwhile()
    for sign in (1, -1):
        for part in range(2):
            arrive(part, ("v", sign, "0"))
            post(part, ("vv", sign, "0"), 0, sign)
    meanwhile()
    for key, name in (("uu+", "2l"), ("uu-", "2h")):
        for part in range(2):
            arrive(part, key)
            post(part, ("v", 1, name), 0, 1)
            post(part, ("v", -1, name), 0, -1)
    meanwhile()
    for name in ("m", "p"):
        for sign in (1, -1):
            for part in range(2):
                arrive(part, ("v", sign, name))
                post(part, ("vv", sign, name), 0, sign)
        meanwhile()
    for sign, name, drop in ((1, "2l", "2h"), (-1, "2h", "2l")):
        for part in range(2):
            arrive(part, ("v", sign, name))
            post(part, ("vv", sign, "2"), 0, sign)
            arrive(part, ("v", -sign, name))
    while work:
        meanwhile()
    for name in ("0", "m", "p", "2"):
        for sign in (1, -1):
            for part in range(2):
                arrive(part, ("vv", sign, name))
    here.wait()
    for k, (source, lo, n, cp) in enumerate(sibs):
        region = coef.at[source + 1 - 2 * c, pl.ds(lo, n)]
        remote(region, region, me, sib_send.at[k], sib_recv.at[k]).wait_recv()
    for cp in sends + [s[3] for s in sibs]:
        cp.wait_send()


def body(own, tiles, owner, local, aux, dom, pair, used, out,
         coef, halves, stage, H, L, partial, sums, take, both, placed1, got,
         g1s, g1r, sbs, sbr, one_sem, st_sem, rs_s, rs_r, b_s, b_r, a1_s, a1_r, a2_s, a2_r, w_s, w_r, loc):
    placed2 = stage.at[1]
    x, y, z, c = coords()
    me = index(x, z, c)

    def plane(d):
        return lax.rem(y + d + 4, 4)

    def peer(dx, d):
        return index(x + dx, z + d // 2, lax.rem(c + d, 2))

    def remote(src, dst, s, r, g, b):
        return pltpu.make_async_remote_copy(src_ref=src, dst_ref=dst, send_sem=s, recv_sem=r,
                                            device_id={"grp": g, "blk": b}, device_id_type=MESH)

    def fetch(m):
        return pltpu.make_async_copy(tiles.at[pl.ds(4 * m, 4)], stage.at[m % 2], st_sem.at[m])

    fetch(0).start()
    fetch(1).start()
    barrier = pltpu.get_barrier_semaphore()
    for d in (1, 2, 3):
        pl.semaphore_signal(barrier, inc=1, device_id={"grp": plane(d), "blk": me}, device_id_type=MESH)

    @pl.loop(1, 32)
    def _(k):
        pl.semaphore_signal(barrier, inc=1, device_id={"grp": y, "blk": peer(k // 8, lax.rem(k, 8))}, device_id_type=MESH)

    pl.semaphore_wait(barrier, 34)

    def halve(m):
        def step():
            fetch(m).wait()

            @pl.loop(0, 32)
            def _(i):
                hi, lo = split(stage[m % 2, i // 8, lax.rem(i, 8)].reshape(128, 128))
                rows = pl.ds(pl.multiple_of(128 * lax.rem(i, 8), 128), 128)
                halves[4 * m + i // 8, rows, 0:128] = hi
                halves[4 * m + i // 8, rows, 128:256] = lo

            if m + 2 < 8:
                fetch(m + 2).start()
        return step

    gather_coeffs(own, coef, (g1s, g1r, sbs, sbr, one_sem), [halve(m) for m in range(8)])

    @pl.loop(0, 8)
    def _(m):
        a = [aux[4 * m + j] for j in range(4)]
        rank = [sum([((a[i] < a[j]) if i > j else (a[i] <= a[j])).astype(jnp.int32) for i in range(4) if i != j]) for j in range(4)]
        at_rank = [[(rank[i] == j).astype(jnp.int32) for i in range(4)] for j in range(4)]
        tile = [4 * m + sum([at_rank[j][i] * i for i in range(4)]) for j in range(4)]
        level = [sum([at_rank[j][i] * a[i] for i in range(4)]) for j in range(4)]
        for j in range(4):
            e = tile[j]
            ch, cl = split(coef[owner[e], local[e]])
            w = jnp.concatenate([ch, cl], axis=1)
            w = jnp.concatenate([w, w], axis=0)
            for q in range(8):
                p = jnp.dot(halves[e, q * 128:(q + 1) * 128, :], w, preferred_element_type=F32)
                p = p[:, :128] + p[:, 128:]
                if j:
                    p += (level[j] == level[j - 1]).astype(F32) * stage[0, j - 1, q].reshape(128, 128)
                stage[0, j, q] = p.reshape(2, 64, 128)
        mask = dom[m].astype(F32)
        rows = pl.ds(pl.multiple_of(128 * m, 128), 128)
        for v in range(4):
            least = sum([(level[j] < v).astype(jnp.int32) for j in range(4)])
            upto = sum([(level[j] <= v).astype(jnp.int32) for j in range(4)])
            on = mask * (upto > least).astype(F32)
            last = jnp.maximum(upto - 1, 0)
            for q in range(8):
                hi, lo = split(stage[0, last, q].reshape(128, 128) * on)
                cols = pl.ds((v * 8 + q) * 128, 128)
                H[rows, cols] = hi
                L[rows, cols] = lo

    def block(I, J, put):
        ri = pl.ds(I * 256, 256)
        rj = pl.ds(J * 256, 256)
        g = lax.dot_general(H[ri, :], H[rj, :], NT, preferred_element_type=F32)
        g += lax.dot_general(L[ri, :], H[rj, :], NT, preferred_element_type=F32)
        g += lax.dot_general(H[ri, :], L[rj, :], NT, preferred_element_type=F32)
        for u in range(2):
            for v in range(2):
                spot, when = put(u, v)

                def store():
                    for half in range(2):
                        at = u * 128 + half * 64
                        partial[spot, half] = g[at:at + 64, v * 128:(v + 1) * 128]
                if when is None:
                    store()
                elif when is not False:
                    pl.when(when)(store)

    rs = []
    for k, (first, count) in enumerate(CHUNKS):
        @pl.loop(0, 2)
        def _(s):
            if k == 0:
                block(s, 3, lambda u, v: (4 * v + 2 * s + u, None))
            elif k == 1:
                block(2 + s, 3, lambda u, v: (8 + 3 * v + 2 * s + u, s < 1 if (u, v) == (1, 0) else None))
            elif k == 2:
                block(s, 2, lambda u, v: (15 + 4 * v + 2 * s + u, None))
            elif k == 3:
                block(2 - 2 * s, 2 - 2 * s, lambda u, v: (23 + 3 * s + u + v, False if (u, v) == (1, 0) else None))
            else:
                block(s, 1, lambda u, v: (29 + 3 * v + 2 * s + u, s < 1 if (u, v) == (1, 0) else None))

        for d in (1, 3, 2):
            cp = remote(partial.at[pl.ds(first, count), :, pl.ds(16 * plane(d), 16), :], sums.at[d - 1, pl.ds(first, count)],
                        rs_s.at[k, d - 1], rs_r.at[k, d - 1], plane(d), me)
            cp.start()
            rs.append(cp)

    mine = pl.ds(pl.multiple_of(16 * y, 16), 16)
    for k, (first, count) in enumerate(CHUNKS):
        for d in range(3):
            region = sums.at[d, pl.ds(first, count)]
            remote(region, region, rs_s.at[k, d], rs_r.at[k, d], y, me).wait_recv()

        @pl.loop(first, first + count)
        def _(q):
            for half in range(2):
                v = (partial[q, half, mine, :] + sums[0, q, half]) + (sums[1, q, half] + sums[2, q, half])
                if half:
                    both[q, mine, :] = v
                else:
                    take[q] = v

    sends = []

    def start(cp):
        cp.start()
        sends.append(cp)

    def done(region, s, r):
        remote(region, region, s, r, y, me).wait_recv()

    def rows(p, base=0):
        return pl.ds(base + pl.multiple_of(16 * p, 16), 16)

    for i, step in enumerate((1, -1)):
        start(remote(both.at[:, mine, :], both.at[:, mine, :], b_s.at[i], b_r.at[i], plane(step), me))

    @pl.loop(0, 64)
    def _(s):
        placed1[s] = take[pair[s]] * used[s].astype(F32)

    def shipment(src, dst, to, s, r):
        return remote(src, dst, s, r, y, to)

    def ship1(dx, d):
        to = peer(dx, d)
        return remote(placed1.at[pl.ds(2 * to, 2)], got.at[pl.ds(2 * me, 2)], a1_s.at[dx, d], a1_r.at[dx, d], y, to)

    def ship2(dx, d):
        to = peer(dx, d)
        return remote(placed2.at[to // 8, lax.rem(to, 8)], out.at[pl.ds(2 * me, 2), 64:128, :], a2_s.at[dx, d], a2_r.at[dx, d], y, to)

    def sender(dx, d):
        return index(x - dx, z - d // 2 + 4, lax.rem(c + d, 2))

    def each(dx, f):
        @pl.loop(1 if dx == 0 else 0, 8)
        def _(d):
            f(dx, d)

    order = (0, 1, 3, 2)
    for dx in order:
        each(dx, lambda dx, d: ship1(dx, d).start())
    own1 = pltpu.make_async_copy(placed1.at[pl.ds(2 * me, 2)], got.at[pl.ds(2 * me, 2)], loc.at[4])
    own1.start()
    for i, step in enumerate((1, -1)):
        done(both.at[:, rows(plane(-step)), :], b_s.at[i], b_r.at[i])
        region = both.at[pl.ds(18 * i, 18), rows(plane(-step)), :]
        start(remote(region, region, b_s.at[2 + i], b_r.at[2 + i], plane(step), me))
    own1.wait()
    locals_ = []
    for dx in order:
        each(dx, lambda dx, d: done(got.at[pl.ds(2 * sender(dx, d), 2)], a1_s.at[dx, d], a1_r.at[dx, d]))
        first = 16 * lax.rem(x - dx + 4, 4)
        for i, step in enumerate((1, -1)):
            start(remote(got.at[pl.ds(first, 16)], out.at[pl.ds(first, 16), rows(y), :], w_s.at[dx, i], w_r.at[dx, i], plane(step), me))
        cp = pltpu.make_async_copy(got.at[pl.ds(first, 16)], out.at[pl.ds(first, 16), rows(y), :], loc.at[dx])
        cp.start()
        locals_.append(cp)
    for i in range(2):
        done(both.at[pl.ds(18 * i, 18), rows(plane(2)), :], b_s.at[2 + i], b_r.at[2 + i])

    @pl.loop(0, 64)
    def _(s):
        placed2[s // 16, lax.rem(s // 2, 8), lax.rem(s, 2)] = both[pair[s]] * used[s].astype(F32)

    for dx in (1, 3, 2, 0):
        each(dx, lambda dx, d: ship2(dx, d).start())
    cp = pltpu.make_async_copy(placed2.at[me // 8, lax.rem(me, 8)], out.at[pl.ds(2 * me, 2), 64:128, :], loc.at[5])
    cp.start()
    locals_.append(cp)
    for dx in order:
        first = 16 * lax.rem(x - dx + 4, 4)
        for i, step in enumerate((1, -1)):
            done(out.at[pl.ds(first, 16), rows(plane(-step)), :], w_s.at[dx, i], w_r.at[dx, i])
            region = out.at[pl.ds(first + 8 * i, 8), rows(plane(-step)), :]
            start(remote(region, region, w_s.at[dx, 2 + i], w_r.at[dx, 2 + i], plane(step), me))
    for dx in order:
        first = 16 * lax.rem(x - dx + 4, 4)
        for i in range(2):
            done(out.at[pl.ds(first + 8 * i, 8), rows(plane(2)), :], w_s.at[dx, 2 + i], w_r.at[dx, 2 + i])
    for dx in order:
        each(dx, lambda dx, d: done(out.at[pl.ds(2 * sender(dx, d), 2), 64:128, :], a2_s.at[dx, d], a2_r.at[dx, d]))
    for cp in locals_:
        cp.wait()
    for cp in rs + sends:
        cp.wait_send()
    for dx in range(4):
        each(dx, lambda dx, d: ship1(dx, d).wait_send())
        each(dx, lambda dx, d: ship2(dx, d).wait_send())


def fused(tiles, coeffs, domains, owner, local, aux, pair, used):
    vm = pl.BlockSpec(memory_space=pltpu.VMEM)
    sm = pl.BlockSpec(memory_space=pltpu.SMEM)
    hbm = pl.BlockSpec(memory_space=pl.ANY)
    dma = pltpu.SemaphoreType.DMA
    return pl.pallas_call(
        body,
        out_shape=jax.ShapeDtypeStruct((64, 128, 128), F32),
        in_specs=[hbm, hbm, sm, sm, sm, vm, sm, sm],
        out_specs=hbm,
        scratch_shapes=[
            pltpu.VMEM((32, 8, 128, 128), F32), pltpu.VMEM((32, 1024, 256), BF16), pltpu.VMEM((2, 4, 8, 2, 64, 128), F32),
            pltpu.VMEM((1024, 4096), BF16), pltpu.VMEM((1024, 4096), BF16),
            pltpu.VMEM((36, 2, 64, 128), F32), pltpu.VMEM((3, 36, 2, 16, 128), F32), pltpu.VMEM((36, 16, 128), F32),
            pltpu.VMEM((36, 64, 128), F32), pltpu.VMEM((64, 16, 128), F32), pltpu.VMEM((64, 16, 128), F32),
            dma((44,)), dma((44,)), dma((45,)), dma((45,)), dma, dma((8,)), dma((5, 3)), dma((5, 3)), dma((4,)), dma((4,)),
            dma((4, 8)), dma((4, 8)), dma((4, 8)), dma((4, 8)), dma((4, 4)), dma((4, 4)), dma((6,))],
        compiler_params=pltpu.CompilerParams(collective_id=1, has_side_effects=True, vmem_limit_bytes=63 * 2**20),
        cost_estimate=pl.CostEstimate(flops=2 * 10**10, bytes_accessed=22 * 10**6, transcendentals=0),
    )(coeffs.reshape(8, 128, 128), tiles.reshape(32, 8, 2, 64, 128), owner, local, aux, domains.reshape(8, 1, 128), pair, used)


def pair_rank(owner):
    at = jnp.arange(owner.shape[0])
    same = (owner[:, None] == owner[None, :]) & (at[None, :] < at[:, None])
    return jnp.sum(same.astype(jnp.int32), axis=1)


def on_device(tiles, coeffs, domains, tile_owner, tile_local, tile_aux, pair_owner):
    targets = pair_owner[:, 0]
    slot = targets * 2 + pair_rank(targets)
    placing = (jnp.arange(64)[:, None] == slot[None, :]).astype(jnp.int32)
    used = jnp.sum(placing, axis=1)
    pair = jnp.sum(placing * jnp.asarray(places())[None, :], axis=1)
    return fused(tiles, coeffs, domains, tile_owner[:, 0], tile_local, tile_aux, pair, used)


def solution(mesh):
    placed = (
        P(("grp", "blk"), None, None, None),
        P("blk", None),
        P("blk", None),
        P(("grp", "blk"), None),
        P(("grp", "blk")),
        P(("grp", "blk")),
        P("blk", None),
    )
    return jax.shard_map(
        on_device, mesh=mesh, in_specs=placed, out_specs=P("blk", None, None), check_vma=False
    )
```

```python
import jax
import jax.numpy as jnp
import numpy as np
from jax import lax
from jax.experimental import pallas as pl
from jax.experimental.pallas import tpu as pltpu
from jax.sharding import PartitionSpec as P

F32, BF16 = jnp.float32, jnp.bfloat16
MESH = pl.DeviceIdType.MESH
NT = (((1,), (1,)), ((), ()))
QUARTERED = ("0",)
CHUNKS = ((0, 8), (8, 7), (15, 8), (23, 6), (29, 7))


def places():
    spot = {}
    for m in range(4):
        for n in (6, 7):
            spot[m, n] = (n - 6) * 4 + m
        for n in (4, 5):
            spot[m, n] = 15 + (n - 4) * 4 + m
    for m in range(4, 8):
        for n in (6, 7):
            spot[m, n] = 8 + 3 * (n - 6) + m - 4
    for s, m in ((0, 4), (1, 0)):
        spot[m, m], spot[m, m + 1], spot[m + 1, m + 1] = 23 + 3 * s, 24 + 3 * s, 25 + 3 * s
    for m in range(4):
        for n in (2, 3):
            spot[m, n] = 29 + 3 * (n - 2) + m
    return np.array([spot[m, n] for m in range(8) for n in range(m, 8)], np.int32)


def split(v):
    hi = v.astype(BF16)
    return hi, (v - hi.astype(F32)).astype(BF16)


def coords():
    b = lax.axis_index("blk")
    return b // 8, lax.axis_index("grp"), lax.rem(b // 2, 4), lax.rem(b, 2)


def index(x, z, c):
    return (lax.rem(x + 8, 4) * 4 + lax.rem(z + 8, 4)) * 2 + c


def gather_coeffs(own, coef, sems, work):
    send, recv, sib_send, sib_recv, y_send, y_recv, local_sem = sems
    x, y, z, c = coords()
    me = index(x, z, c)
    other = index(x, z, 1 - c)
    axes = [((1, 0), (0, 1)), ((0, 1), (1, 0))]

    def at(part, du, dv):
        (ux, uz), (vx, vz) = axes[part]
        return index(x + du * ux + dv * vx, z + du * uz + dv * vz, c)

    here = pltpu.make_async_copy(own, coef.at[me], local_sem)
    here.start()
    sends, sibs = [], []

    def remote(src, dst, to, s, r):
        return pltpu.make_async_remote_copy(src_ref=src, dst_ref=dst, send_sem=s, recv_sem=r,
                                            device_id={"grp": y, "blk": to}, device_id_type=MESH)

    def sibling(source, lo, n, src=None):
        k = len(sibs)
        region = coef.at[source, pl.ds(lo, n)]
        cp = remote(region if src is None else src, region, other, sib_send.at[k], sib_recv.at[k])
        cp.start()
        sibs.append((source, lo, n, cp))

    table = {}

    def define(part, key, du, dv, lo, n):
        quarter = key[0] in ("v", "vv") and key[2] in QUARTERED
        if not quarter:
            table[part, key] = (len(table), du, dv, lambda ref: ref.at[pl.ds(part * 4 + lo, n)], (part * 4 + lo, n))
        elif key[0] == "v":
            table[part, key] = (len(table), du, dv, lambda ref: ref.at[part * 4 + y], None)
        else:
            table[part, key] = (len(table), du, dv, lambda ref: ref.at[part * 4 + y, pl.ds(32 * lo, 64)], None)

    for part in range(2):
        define(part, "u+", -1, 0, 0, 4)
        define(part, "u-", 1, 0, 0, 4)
        define(part, "uu+", -2, 0, 0, 2)
        define(part, "uu-", 2, 0, 2, 2)
        for sign in (1, -1):
            for name, du, lo, n in (("0", 0, 0, 4), ("m", -1, 0, 4), ("p", 1, 0, 4), ("2l", 2, 0, 2), ("2h", 2, 2, 2)):
                define(part, ("v", sign, name), du, -sign, lo, n)
            for name, du in (("0", 0), ("m", -1), ("p", 1), ("2", 2)):
                define(part, ("vv", sign, name), du, -2 * sign, 0 if sign > 0 else 2, 2)

    def post(part, key, du_to, dv_to, src=None):
        k, du, dv, blocks, share = table[part, key]
        region = blocks(coef.at[at(part, du + du_to, dv + dv_to)])
        cp = remote(region if src is None else blocks(src), region, at(part, du_to, dv_to), send.at[k], recv.at[k])
        cp.start()
        sends.append(cp)

    def arrive(part, key):
        k, du, dv, blocks, share = table[part, key]
        source = at(part, du, dv)
        region = blocks(coef.at[source])
        remote(region, region, me, send.at[k], recv.at[k]).wait_recv()
        if share:
            sibling(source, *share)

    def plane(d):
        return lax.rem(y + d + 4, 4)

    def swap(part, name, dv, i, block, half, to, sem):
        source = at(part, {"0": 0, "m": -1}[name], dv)
        k = (part * len(QUARTERED) + QUARTERED.index(name)) * 3 + dv % 4 - 1
        region = coef.at[source, part * 4 + block]
        if half:
            region = region.at[pl.ds(64 * i, 64)]
        return pltpu.make_async_remote_copy(src_ref=region, dst_ref=region, send_sem=y_send.at[k, sem], recv_sem=y_recv.at[k, sem],
                                            device_id={"grp": to, "blk": me}, device_id_type=MESH)

    def swap_start(name, dv):
        for part in range(2):
            for i, step in enumerate((1, -1)):
                cp = swap(part, name, dv, i, y, False, plane(step), i)
                cp.start()
                sends.append(cp)

    def swap_on(name, dv):
        for part in range(2):
            for i, step in enumerate((1, -1)):
                swap(part, name, dv, i, plane(-step), False, y, i).wait_recv()
                cp = swap(part, name, dv, i, plane(-step), True, plane(step), 2 + i)
                cp.start()
                sends.append(cp)

    def swap_end(name, dv):
        for part in range(2):
            for i in range(2):
                swap(part, name, dv, i, plane(2), True, y, 2 + i).wait_recv()
            sibling(at(part, {"0": 0, "m": -1}[name], dv), part * 4, 4)

    def quartered(name, f, *dvs):
        if name in QUARTERED:
            for dv in dvs:
                f(name, dv)

    def meanwhile():
        if work:
            work.pop(0)()

    for part in range(2):
        post(part, "u+", 1, 0, own)
        post(part, "u-", -1, 0, own)
    for part in range(2):
        post(part, ("v", 1, "0"), 0, 1, own)
        post(part, ("v", -1, "0"), 0, -1, own)
    sibling(me, 0, 8, own)
    meanwhile()
    meanwhile()
    for key, name, fwd, step in (("u+", "m", "uu+", 1), ("u-", "p", "uu-", -1)):
        for part in range(2):
            arrive(part, key)
            post(part, fwd, step, 0)
            post(part, ("v", 1, name), 0, 1)
            post(part, ("v", -1, name), 0, -1)
    meanwhile()
    for sign in (1, -1):
        for part in range(2):
            arrive(part, ("v", sign, "0"))
            post(part, ("vv", sign, "0"), 0, sign)
    quartered("0", swap_start, 1, -1)
    meanwhile()
    for key, name in (("uu+", "2l"), ("uu-", "2h")):
        for part in range(2):
            arrive(part, key)
            post(part, ("v", 1, name), 0, 1)
            post(part, ("v", -1, name), 0, -1)
    meanwhile()
    for sign in (1, -1):
        for part in range(2):
            arrive(part, ("v", sign, "m"))
            post(part, ("vv", sign, "m"), 0, sign)
    quartered("m", swap_start, 1, -1)
    meanwhile()
    for sign in (1, -1):
        for part in range(2):
            arrive(part, ("vv", sign, "0"))
    quartered("0", swap_start, 2)
    quartered("0", swap_on, 1, -1)
    for sign in (1, -1):
        for part in range(2):
            arrive(part, ("v", sign, "p"))
            post(part, ("vv", sign, "p"), 0, sign)
    meanwhile()
    for sign in (1, -1):
        for part in range(2):
            arrive(part, ("vv", sign, "m"))
    quartered("m", swap_start, 2)
    quartered("0", swap_end, 1, -1)
    quartered("0", swap_on, 2)
    quartered("m", swap_on, 1, -1)
    for sign, name, drop in ((1, "2l", "2h"), (-1, "2h", "2l")):
        for part in range(2):
            arrive(part, ("v", sign, name))
            post(part, ("vv", sign, "2"), 0, sign)
            arrive(part, ("v", -sign, name))
    while work:
        meanwhile()
    quartered("m", swap_on, 2)
    quartered("0", swap_end, 2)
    quartered("m", swap_end, 1, -1)
    for name in ("p", "2"):
        for sign in (1, -1):
            for part in range(2):
                arrive(part, ("vv", sign, name))
    quartered("m", swap_end, 2)
    here.wait()
    for k, (source, lo, n, cp) in enumerate(sibs):
        region = coef.at[source + 1 - 2 * c, pl.ds(lo, n)]
        remote(region, region, me, sib_send.at[k], sib_recv.at[k]).wait_recv()
    for cp in sends + [s[3] for s in sibs]:
        cp.wait_send()


def body(own, tiles, owner, local, aux, dom, first_pair, last_pair, out,
         coef, halves, stage, H, L, partial, sums, take, both, placed1, got,
         g1s, g1r, sbs, sbr, ys, yr, one_sem, st_sem, rs_s, rs_r, b_s, b_r, a1_s, a1_r, a2_s, a2_r, w_s, w_r, loc):
    placed2 = stage.at[1]
    x, y, z, c = coords()
    me = index(x, z, c)

    def plane(d):
        return lax.rem(y + d + 4, 4)

    def peer(dx, d):
        return index(x + dx, z + d // 2, lax.rem(c + d, 2))

    def remote(src, dst, s, r, g, b):
        return pltpu.make_async_remote_copy(src_ref=src, dst_ref=dst, send_sem=s, recv_sem=r,
                                            device_id={"grp": g, "blk": b}, device_id_type=MESH)

    def fetch(m):
        return pltpu.make_async_copy(tiles.at[pl.ds(4 * m, 4)], stage.at[m % 2], st_sem.at[m])

    fetch(0).start()
    fetch(1).start()
    barrier = pltpu.get_barrier_semaphore()
    for g, b in ((plane(1), me), (plane(-1), me), (plane(2), me), (y, index(x, z, 1 - c)), (y, index(x + 1, z, c)),
                 (y, index(x - 1, z, c)), (y, index(x, z + 1, c)), (y, index(x, z - 1, c))):
        pl.semaphore_signal(barrier, inc=1, device_id={"grp": g, "blk": b}, device_id_type=MESH)
    pl.semaphore_wait(barrier, 8)

    def halve(m):
        def step():
            fetch(m).wait()

            @pl.loop(0, 32)
            def _(i):
                hi, lo = split(stage[m % 2, i // 8, lax.rem(i, 8)].reshape(128, 128))
                rows = pl.ds(pl.multiple_of(128 * lax.rem(i, 8), 128), 128)
                halves[4 * m + i // 8, rows, 0:128] = hi
                halves[4 * m + i // 8, rows, 128:256] = lo

            if m + 2 < 8:
                fetch(m + 2).start()
        return step

    gather_coeffs(own, coef, (g1s, g1r, sbs, sbr, ys, yr, one_sem), [halve(m) for m in range(8)])

    @pl.loop(0, 8)
    def _(m):
        a = [aux[4 * m + j] for j in range(4)]
        rank = [sum([((a[i] < a[j]) if i > j else (a[i] <= a[j])).astype(jnp.int32) for i in range(4) if i != j]) for j in range(4)]
        at_rank = [[(rank[i] == j).astype(jnp.int32) for i in range(4)] for j in range(4)]
        tile = [4 * m + sum([at_rank[j][i] * i for i in range(4)]) for j in range(4)]
        level = [sum([at_rank[j][i] * a[i] for i in range(4)]) for j in range(4)]
        for j in range(4):
            e = tile[j]
            ch, cl = split(coef[owner[e], local[e]])
            w = jnp.concatenate([ch, cl], axis=1)
            w = jnp.concatenate([w, w], axis=0)
            for q in range(8):
                p = jnp.dot(halves[e, q * 128:(q + 1) * 128, :], w, preferred_element_type=F32)
                p = p[:, :128] + p[:, 128:]
                if j:
                    p += (level[j] == level[j - 1]).astype(F32) * stage[0, j - 1, q].reshape(128, 128)
                stage[0, j, q] = p.reshape(2, 64, 128)
        mask = dom[m].astype(F32)
        rows = pl.ds(pl.multiple_of(128 * m, 128), 128)
        for v in range(4):
            least = sum([(level[j] < v).astype(jnp.int32) for j in range(4)])
            upto = sum([(level[j] <= v).astype(jnp.int32) for j in range(4)])
            on = mask * (upto > least).astype(F32)
            last = jnp.maximum(upto - 1, 0)
            for q in range(8):
                hi, lo = split(stage[0, last, q].reshape(128, 128) * on)
                cols = pl.ds((v * 8 + q) * 128, 128)
                H[rows, cols] = hi
                L[rows, cols] = lo

    def block(I, J, put):
        ri = pl.ds(I * 256, 256)
        rj = pl.ds(J * 256, 256)
        g = lax.dot_general(H[ri, :], H[rj, :], NT, preferred_element_type=F32)
        g += lax.dot_general(L[ri, :], H[rj, :], NT, preferred_element_type=F32)
        g += lax.dot_general(H[ri, :], L[rj, :], NT, preferred_element_type=F32)
        for u in range(2):
            for v in range(2):
                spot, when = put(u, v)

                def store():
                    for half in range(2):
                        at = u * 128 + half * 64
                        partial[spot, half] = g[at:at + 64, v * 128:(v + 1) * 128]
                if when is None:
                    store()
                elif when is not False:
                    pl.when(when)(store)

    rs = []
    for k, (first, count) in enumerate(CHUNKS):
        @pl.loop(0, 2)
        def _(s):
            if k == 0:
                block(s, 3, lambda u, v: (4 * v + 2 * s + u, None))
            elif k == 1:
                block(2 + s, 3, lambda u, v: (8 + 3 * v + 2 * s + u, s < 1 if (u, v) == (1, 0) else None))
            elif k == 2:
                block(s, 2, lambda u, v: (15 + 4 * v + 2 * s + u, None))
            elif k == 3:
                block(2 - 2 * s, 2 - 2 * s, lambda u, v: (23 + 3 * s + u + v, False if (u, v) == (1, 0) else None))
            else:
                block(s, 1, lambda u, v: (29 + 3 * v + 2 * s + u, s < 1 if (u, v) == (1, 0) else None))

        for d in (1, 3, 2):
            cp = remote(partial.at[pl.ds(first, count), :, pl.ds(16 * plane(d), 16), :], sums.at[d - 1, pl.ds(first, count)],
                        rs_s.at[k, d - 1], rs_r.at[k, d - 1], plane(d), me)
            cp.start()
            rs.append(cp)

    mine = pl.ds(pl.multiple_of(16 * y, 16), 16)
    for k, (first, count) in enumerate(CHUNKS):
        for d in range(3):
            region = sums.at[d, pl.ds(first, count)]
            remote(region, region, rs_s.at[k, d], rs_r.at[k, d], y, me).wait_recv()

        @pl.loop(first, first + count)
        def _(q):
            for half in range(2):
                v = (partial[q, half, mine, :] + sums[0, q, half]) + (sums[1, q, half] + sums[2, q, half])
                if half:
                    both[q, mine, :] = v
                else:
                    take[q] = v

    sends = []

    def start(cp):
        cp.start()
        sends.append(cp)

    def done(region, s, r):
        remote(region, region, s, r, y, me).wait_recv()

    def rows(p, base=0):
        return pl.ds(base + pl.multiple_of(16 * p, 16), 16)

    for i, step in enumerate((1, -1)):
        start(remote(both.at[:, mine, :], both.at[:, mine, :], b_s.at[i], b_r.at[i], plane(step), me))

    def slot(s):
        o = s // 2
        second = lax.rem(s, 2)
        early, late = first_pair[o], last_pair[o]
        spot = lax.rem(jnp.maximum(jnp.where(second == 1, late, early), 0), 64)
        return spot, jnp.where(second == 1, late > early, early < 4096).astype(F32)

    @pl.loop(0, 64)
    def _(s):
        spot, filled = slot(s)
        placed1[s] = take[spot] * filled

    def shipment(src, dst, to, s, r):
        return remote(src, dst, s, r, y, to)

    def ship1(dx, d):
        to = peer(dx, d)
        return remote(placed1.at[pl.ds(2 * to, 2)], got.at[pl.ds(2 * me, 2)], a1_s.at[dx, d], a1_r.at[dx, d], y, to)

    def ship2(dx, d):
        to = peer(dx, d)
        return remote(placed2.at[to // 8, lax.rem(to, 8)], out.at[pl.ds(2 * me, 2), 64:128, :], a2_s.at[dx, d], a2_r.at[dx, d], y, to)

    def sender(dx, d):
        return index(x - dx, z - d // 2 + 4, lax.rem(c + d, 2))

    def each(dx, f):
        @pl.loop(1 if dx == 0 else 0, 8)
        def _(d):
            f(dx, d)

    order = (0, 1, 3, 2)
    for dx in order:
        each(dx, lambda dx, d: ship1(dx, d).start())
    own1 = pltpu.make_async_copy(placed1.at[pl.ds(2 * me, 2)], got.at[pl.ds(2 * me, 2)], loc.at[4])
    own1.start()
    for i, step in enumerate((1, -1)):
        done(both.at[:, rows(plane(-step)), :], b_s.at[i], b_r.at[i])
        region = both.at[pl.ds(18 * i, 18), rows(plane(-step)), :]
        start(remote(region, region, b_s.at[2 + i], b_r.at[2 + i], plane(step), me))
    own1.wait()
    locals_ = []
    for dx in order:
        each(dx, lambda dx, d: done(got.at[pl.ds(2 * sender(dx, d), 2)], a1_s.at[dx, d], a1_r.at[dx, d]))
        first = 16 * lax.rem(x - dx + 4, 4)
        for i, step in enumerate((1, -1)):
            start(remote(got.at[pl.ds(first, 16)], out.at[pl.ds(first, 16), rows(y), :], w_s.at[dx, i], w_r.at[dx, i], plane(step), me))
        cp = pltpu.make_async_copy(got.at[pl.ds(first, 16)], out.at[pl.ds(first, 16), rows(y), :], loc.at[dx])
        cp.start()
        locals_.append(cp)
    for i in range(2):
        done(both.at[pl.ds(18 * i, 18), rows(plane(2)), :], b_s.at[2 + i], b_r.at[2 + i])

    @pl.loop(0, 64)
    def _(s):
        spot, filled = slot(s)
        placed2[s // 16, lax.rem(s // 2, 8), lax.rem(s, 2)] = both[spot] * filled

    for dx in (1, 3, 2, 0):
        each(dx, lambda dx, d: ship2(dx, d).start())
    cp = pltpu.make_async_copy(placed2.at[me // 8, lax.rem(me, 8)], out.at[pl.ds(2 * me, 2), 64:128, :], loc.at[5])
    cp.start()
    locals_.append(cp)
    for dx in order:
        first = 16 * lax.rem(x - dx + 4, 4)
        for i, step in enumerate((1, -1)):
            done(out.at[pl.ds(first, 16), rows(plane(-step)), :], w_s.at[dx, i], w_r.at[dx, i])
            region = out.at[pl.ds(first + 8 * i, 8), rows(plane(-step)), :]
            start(remote(region, region, w_s.at[dx, 2 + i], w_r.at[dx, 2 + i], plane(step), me))
    for dx in order:
        first = 16 * lax.rem(x - dx + 4, 4)
        for i in range(2):
            done(out.at[pl.ds(first + 8 * i, 8), rows(plane(2)), :], w_s.at[dx, 2 + i], w_r.at[dx, 2 + i])
    for dx in order:
        each(dx, lambda dx, d: done(out.at[pl.ds(2 * sender(dx, d), 2), 64:128, :], a2_s.at[dx, d], a2_r.at[dx, d]))
    for cp in locals_:
        cp.wait()
    for cp in rs + sends:
        cp.wait_send()
    for dx in range(4):
        each(dx, lambda dx, d: ship1(dx, d).wait_send())
        each(dx, lambda dx, d: ship2(dx, d).wait_send())


def fused(tiles, coeffs, domains, owner, local, aux, first_pair, last_pair):
    vm = pl.BlockSpec(memory_space=pltpu.VMEM)
    sm = pl.BlockSpec(memory_space=pltpu.SMEM)
    hbm = pl.BlockSpec(memory_space=pl.ANY)
    dma = pltpu.SemaphoreType.DMA
    return pl.pallas_call(
        body,
        out_shape=jax.ShapeDtypeStruct((64, 128, 128), F32),
        in_specs=[hbm, hbm, sm, sm, sm, vm, sm, sm],
        out_specs=hbm,
        scratch_shapes=[
            pltpu.VMEM((32, 8, 128, 128), F32), pltpu.VMEM((32, 1024, 256), BF16), pltpu.VMEM((2, 4, 8, 2, 64, 128), F32),
            pltpu.VMEM((1024, 4096), BF16), pltpu.VMEM((1024, 4096), BF16),
            pltpu.VMEM((36, 2, 64, 128), F32), pltpu.VMEM((3, 36, 2, 16, 128), F32), pltpu.VMEM((36, 16, 128), F32),
            pltpu.VMEM((36, 64, 128), F32), pltpu.VMEM((64, 16, 128), F32), pltpu.VMEM((64, 16, 128), F32),
            dma((44,)), dma((44,)), dma((45,)), dma((45,)), dma((6 * len(QUARTERED), 4)), dma((6 * len(QUARTERED), 4)), dma,
            dma((8,)), dma((5, 3)), dma((5, 3)), dma((4,)), dma((4,)),
            dma((4, 8)), dma((4, 8)), dma((4, 8)), dma((4, 8)), dma((4, 4)), dma((4, 4)), dma((6,))],
        compiler_params=pltpu.CompilerParams(collective_id=1, has_side_effects=True, vmem_limit_bytes=63 * 2**20),
        cost_estimate=pl.CostEstimate(flops=2 * 10**10, bytes_accessed=22 * 10**6, transcendentals=0),
    )(coeffs.reshape(8, 128, 128), tiles.reshape(32, 8, 2, 64, 128), owner, local, aux, domains.reshape(8, 1, 128), first_pair, last_pair)


def on_device(tiles, coeffs, domains, tile_owner, tile_local, tile_aux, pair_owner):
    named = pair_owner[:, 0][None, :] == jnp.arange(32)[:, None]
    code = jnp.asarray(np.arange(36, dtype=np.int32) * 64 + places())[None, :]
    first_pair = jnp.min(jnp.where(named, code, 4096), axis=1)
    last_pair = jnp.max(jnp.where(named, code, -1), axis=1)
    return fused(tiles, coeffs, domains, tile_owner[:, 0], tile_local, tile_aux, first_pair, last_pair)


def solution(mesh):
    placed = (
        P(("grp", "blk"), None, None, None),
        P("blk", None),
        P("blk", None),
        P(("grp", "blk"), None),
        P(("grp", "blk")),
        P(("grp", "blk")),
        P("blk", None),
    )
    return jax.shard_map(
        on_device, mesh=mesh, in_specs=placed, out_specs=P("blk", None, None), check_vma=False
    )
```

```python
import jax
import jax.numpy as jnp
import numpy as np
from jax import lax
from jax.experimental import pallas as pl
from jax.experimental.pallas import tpu as pltpu
from jax.sharding import PartitionSpec as P

F32, BF16 = jnp.float32, jnp.bfloat16
MESH = pl.DeviceIdType.MESH
NT = (((1,), (1,)), ((), ()))
QUARTERED = ("0",)
CHUNKS = ((0, 8), (8, 7), (15, 8), (23, 6), (29, 7))


def places():
    spot = {}
    for m in range(4):
        for n in (6, 7):
            spot[m, n] = (n - 6) * 4 + m
        for n in (4, 5):
            spot[m, n] = 15 + (n - 4) * 4 + m
    for m in range(4, 8):
        for n in (6, 7):
            spot[m, n] = 8 + 3 * (n - 6) + m - 4
    for s, m in ((0, 4), (1, 0)):
        spot[m, m], spot[m, m + 1], spot[m + 1, m + 1] = 23 + 3 * s, 24 + 3 * s, 25 + 3 * s
    for m in range(4):
        for n in (2, 3):
            spot[m, n] = 29 + 3 * (n - 2) + m
    return np.array([spot[m, n] for m in range(8) for n in range(m, 8)], np.int32)


def split(v):
    hi = v.astype(BF16)
    return hi, (v - hi.astype(F32)).astype(BF16)


def coords():
    b = lax.axis_index("blk")
    return b // 8, lax.axis_index("grp"), lax.rem(b // 2, 4), lax.rem(b, 2)


def index(x, z, c):
    return (lax.rem(x + 8, 4) * 4 + lax.rem(z + 8, 4)) * 2 + c


def gather_coeffs(own, coef, sems, work):
    send, recv, sib_send, sib_recv, y_send, y_recv, local_sem = sems
    x, y, z, c = coords()
    me = index(x, z, c)
    other = index(x, z, 1 - c)
    axes = [((1, 0), (0, 1)), ((0, 1), (1, 0))]

    def at(part, du, dv):
        (ux, uz), (vx, vz) = axes[part]
        return index(x + du * ux + dv * vx, z + du * uz + dv * vz, c)

    here = pltpu.make_async_copy(own, coef.at[me], local_sem)
    here.start()
    sends, sibs = [], []

    def remote(src, dst, to, s, r):
        return pltpu.make_async_remote_copy(src_ref=src, dst_ref=dst, send_sem=s, recv_sem=r,
                                            device_id={"grp": y, "blk": to}, device_id_type=MESH)

    def sibling(source, lo, n, src=None):
        k = len(sibs)
        region = coef.at[source, pl.ds(lo, n)]
        cp = remote(region if src is None else src, region, other, sib_send.at[k], sib_recv.at[k])
        cp.start()
        sibs.append((source, lo, n, cp))

    table = {}

    def define(part, key, du, dv, lo, n):
        quarter = key[0] in ("v", "vv") and key[2] in QUARTERED
        if not quarter:
            table[part, key] = (len(table), du, dv, lambda ref: ref.at[pl.ds(part * 4 + lo, n)], (part * 4 + lo, n))
        elif key[0] == "v":
            table[part, key] = (len(table), du, dv, lambda ref: ref.at[part * 4 + y], None)
        else:
            table[part, key] = (len(table), du, dv, lambda ref: ref.at[part * 4 + y, pl.ds(32 * lo, 64)], None)

    for part in range(2):
        define(part, "u+", -1, 0, 0, 4)
        define(part, "u-", 1, 0, 0, 4)
        define(part, "uu+", -2, 0, 0, 2)
        define(part, "uu-", 2, 0, 2, 2)
        for sign in (1, -1):
            for name, du, lo, n in (("0", 0, 0, 4), ("m", -1, 0, 4), ("p", 1, 0, 4), ("2l", 2, 0, 2), ("2h", 2, 2, 2)):
                define(part, ("v", sign, name), du, -sign, lo, n)
            for name, du in (("0", 0), ("m", -1), ("p", 1), ("2", 2)):
                define(part, ("vv", sign, name), du, -2 * sign, 0 if sign > 0 else 2, 2)

    def post(part, key, du_to, dv_to, src=None):
        k, du, dv, blocks, share = table[part, key]
        region = blocks(coef.at[at(part, du + du_to, dv + dv_to)])
        cp = remote(region if src is None else blocks(src), region, at(part, du_to, dv_to), send.at[k], recv.at[k])
        cp.start()
        sends.append(cp)

    def arrive(part, key):
        k, du, dv, blocks, share = table[part, key]
        source = at(part, du, dv)
        region = blocks(coef.at[source])
        remote(region, region, me, send.at[k], recv.at[k]).wait_recv()
        if share:
            sibling(source, *share)

    def plane(d):
        return lax.rem(y + d + 4, 4)

    def swap(part, name, dv, i, block, half, to, sem):
        source = at(part, {"0": 0, "m": -1}[name], dv)
        k = (part * len(QUARTERED) + QUARTERED.index(name)) * 3 + dv % 4 - 1
        region = coef.at[source, part * 4 + block]
        if half:
            region = region.at[pl.ds(64 * i, 64)]
        return pltpu.make_async_remote_copy(src_ref=region, dst_ref=region, send_sem=y_send.at[k, sem], recv_sem=y_recv.at[k, sem],
                                            device_id={"grp": to, "blk": me}, device_id_type=MESH)

    def swap_start(name, dv):
        for part in range(2):
            for i, step in enumerate((1, -1)):
                cp = swap(part, name, dv, i, y, False, plane(step), i)
                cp.start()
                sends.append(cp)

    def swap_on(name, dv):
        for part in range(2):
            for i, step in enumerate((1, -1)):
                swap(part, name, dv, i, plane(-step), False, y, i).wait_recv()
                cp = swap(part, name, dv, i, plane(-step), True, plane(step), 2 + i)
                cp.start()
                sends.append(cp)

    def swap_end(name, dv):
        for part in range(2):
            for i in range(2):
                swap(part, name, dv, i, plane(2), True, y, 2 + i).wait_recv()
            sibling(at(part, {"0": 0, "m": -1}[name], dv), part * 4, 4)

    def quartered(name, f, *dvs):
        if name in QUARTERED:
            for dv in dvs:
                f(name, dv)

    def meanwhile():
        if work:
            work.pop(0)()

    for part in range(2):
        post(part, "u+", 1, 0, own)
        post(part, "u-", -1, 0, own)
    for part in range(2):
        post(part, ("v", 1, "0"), 0, 1, own)
        post(part, ("v", -1, "0"), 0, -1, own)
    sibling(me, 0, 8, own)
    meanwhile()
    meanwhile()
    for key, name, fwd, step in (("u+", "m", "uu+", 1), ("u-", "p", "uu-", -1)):
        for part in range(2):
            arrive(part, key)
            post(part, fwd, step, 0)
            post(part, ("v", 1, name), 0, 1)
            post(part, ("v", -1, name), 0, -1)
    meanwhile()
    for sign in (1, -1):
        for part in range(2):
            arrive(part, ("v", sign, "0"))
            post(part, ("vv", sign, "0"), 0, sign)
    quartered("0", swap_start, 1, -1)
    meanwhile()
    for key, name in (("uu+", "2l"), ("uu-", "2h")):
        for part in range(2):
            arrive(part, key)
            post(part, ("v", 1, name), 0, 1)
            post(part, ("v", -1, name), 0, -1)
    meanwhile()
    for sign in (1, -1):
        for part in range(2):
            arrive(part, ("v", sign, "m"))
            post(part, ("vv", sign, "m"), 0, sign)
    quartered("m", swap_start, 1, -1)
    meanwhile()
    for sign in (1, -1):
        for part in range(2):
            arrive(part, ("vv", sign, "0"))
    quartered("0", swap_start, 2)
    quartered("0", swap_on, 1, -1)
    for sign in (1, -1):
        for part in range(2):
            arrive(part, ("v", sign, "p"))
            post(part, ("vv", sign, "p"), 0, sign)
    meanwhile()
    for sign in (1, -1):
        for part in range(2):
            arrive(part, ("vv", sign, "m"))
    quartered("m", swap_start, 2)
    quartered("0", swap_end, 1, -1)
    quartered("0", swap_on, 2)
    quartered("m", swap_on, 1, -1)
    for sign, name, drop in ((1, "2l", "2h"), (-1, "2h", "2l")):
        for part in range(2):
            arrive(part, ("v", sign, name))
            post(part, ("vv", sign, "2"), 0, sign)
            arrive(part, ("v", -sign, name))
    while work:
        meanwhile()
    quartered("m", swap_on, 2)
    quartered("0", swap_end, 2)
    quartered("m", swap_end, 1, -1)
    for name in ("p", "2"):
        for sign in (1, -1):
            for part in range(2):
                arrive(part, ("vv", sign, name))
    quartered("m", swap_end, 2)
    here.wait()
    for k, (source, lo, n, cp) in enumerate(sibs):
        region = coef.at[source + 1 - 2 * c, pl.ds(lo, n)]
        remote(region, region, me, sib_send.at[k], sib_recv.at[k]).wait_recv()
    for cp in sends + [s[3] for s in sibs]:
        cp.wait_send()


def body(own, tiles, owner, local, aux, dom, first_pair, last_pair, out,
         coef, halves, stage, H, L, partial, sums, take, both0, both1, placed1, got,
         g1s, g1r, sbs, sbr, ys, yr, one_sem, st_sem, rs_s, rs_r, b_s, b_r, a1_s, a1_r, a2_s, a2_r, w_s, w_r, loc):
    placed2 = stage.at[1]
    both = both0, both1
    x, y, z, c = coords()
    me = index(x, z, c)

    def plane(d):
        return lax.rem(y + d + 4, 4)

    def peer(dx, d):
        return index(x + dx, z + d // 2, lax.rem(c + d, 2))

    def remote(src, dst, s, r, g, b):
        return pltpu.make_async_remote_copy(src_ref=src, dst_ref=dst, send_sem=s, recv_sem=r,
                                            device_id={"grp": g, "blk": b}, device_id_type=MESH)

    def fetch(m):
        return pltpu.make_async_copy(tiles.at[pl.ds(4 * m, 4)], stage.at[m % 2], st_sem.at[m])

    fetch(0).start()
    fetch(1).start()
    barrier = pltpu.get_barrier_semaphore()
    for g, b in ((plane(1), me), (plane(-1), me), (plane(2), me), (y, index(x, z, 1 - c)), (y, index(x + 1, z, c)),
                 (y, index(x - 1, z, c)), (y, index(x, z + 1, c)), (y, index(x, z - 1, c))):
        pl.semaphore_signal(barrier, inc=1, device_id={"grp": g, "blk": b}, device_id_type=MESH)
    pl.semaphore_wait(barrier, 8)

    def halve(m):
        def step():
            fetch(m).wait()

            @pl.loop(0, 32)
            def _(i):
                hi, lo = split(stage[m % 2, i // 8, lax.rem(i, 8)].reshape(128, 128))
                rows = pl.ds(pl.multiple_of(128 * lax.rem(i, 8), 128), 128)
                halves[4 * m + i // 8, rows, 0:128] = hi
                halves[4 * m + i // 8, rows, 128:256] = lo

            if m + 2 < 8:
                fetch(m + 2).start()
        return step

    gather_coeffs(own, coef, (g1s, g1r, sbs, sbr, ys, yr, one_sem), [halve(m) for m in range(8)])

    @pl.loop(0, 8)
    def _(m):
        a = [aux[4 * m + j] for j in range(4)]
        rank = [sum([((a[i] < a[j]) if i > j else (a[i] <= a[j])).astype(jnp.int32) for i in range(4) if i != j]) for j in range(4)]
        at_rank = [[(rank[i] == j).astype(jnp.int32) for i in range(4)] for j in range(4)]
        tile = [4 * m + sum([at_rank[j][i] * i for i in range(4)]) for j in range(4)]
        level = [sum([at_rank[j][i] * a[i] for i in range(4)]) for j in range(4)]
        for j in range(4):
            e = tile[j]
            ch, cl = split(coef[owner[e], local[e]])
            w = jnp.concatenate([ch, cl], axis=1)
            w = jnp.concatenate([w, w], axis=0)
            for q in range(8):
                p = jnp.dot(halves[e, q * 128:(q + 1) * 128, :], w, preferred_element_type=F32)
                p = p[:, :128] + p[:, 128:]
                if j:
                    p += (level[j] == level[j - 1]).astype(F32) * stage[0, j - 1, q].reshape(128, 128)
                stage[0, j, q] = p.reshape(2, 64, 128)
        mask = dom[m].astype(F32)
        rows = pl.ds(pl.multiple_of(128 * m, 128), 128)
        for v in range(4):
            least = sum([(level[j] < v).astype(jnp.int32) for j in range(4)])
            upto = sum([(level[j] <= v).astype(jnp.int32) for j in range(4)])
            on = mask * (upto > least).astype(F32)
            last = jnp.maximum(upto - 1, 0)
            for q in range(8):
                hi, lo = split(stage[0, last, q].reshape(128, 128) * on)
                cols = pl.ds((v * 8 + q) * 128, 128)
                H[rows, cols] = hi
                L[rows, cols] = lo

    def block(I, J, put):
        ri = pl.ds(I * 256, 256)
        rj = pl.ds(J * 256, 256)
        g = lax.dot_general(H[ri, :], H[rj, :], NT, preferred_element_type=F32)
        g += lax.dot_general(L[ri, :], H[rj, :], NT, preferred_element_type=F32)
        g += lax.dot_general(H[ri, :], L[rj, :], NT, preferred_element_type=F32)
        for u in range(2):
            for v in range(2):
                spot, when = put(u, v)

                def store():
                    cols = slice(v * 128, (v + 1) * 128)
                    partial[spot, 0] = g[u * 128:u * 128 + 64, cols]
                    for p in range(4):
                        for t in range(2):
                            at = u * 128 + 64 + 32 * t + 8 * p
                            partial[spot, 1, 16 * p + 8 * t:16 * p + 8 * t + 8, :] = g[at:at + 8, cols]
                if when is None:
                    store()
                elif when is not False:
                    pl.when(when)(store)

    rs = []
    for k, (first, count) in enumerate(CHUNKS):
        @pl.loop(0, 2)
        def _(s):
            if k == 0:
                block(s, 3, lambda u, v: (4 * v + 2 * s + u, None))
            elif k == 1:
                block(2 + s, 3, lambda u, v: (8 + 3 * v + 2 * s + u, s < 1 if (u, v) == (1, 0) else None))
            elif k == 2:
                block(s, 2, lambda u, v: (15 + 4 * v + 2 * s + u, None))
            elif k == 3:
                block(2 - 2 * s, 2 - 2 * s, lambda u, v: (23 + 3 * s + u + v, False if (u, v) == (1, 0) else None))
            else:
                block(s, 1, lambda u, v: (29 + 3 * v + 2 * s + u, s < 1 if (u, v) == (1, 0) else None))

        for d in (1, 3, 2):
            cp = remote(partial.at[pl.ds(first, count), :, pl.ds(16 * plane(d), 16), :], sums.at[d - 1, pl.ds(first, count)],
                        rs_s.at[k, d - 1], rs_r.at[k, d - 1], plane(d), me)
            cp.start()
            rs.append(cp)

    mine = pl.ds(pl.multiple_of(16 * y, 16), 16)
    for k, (first, count) in enumerate(CHUNKS):
        for d in range(3):
            region = sums.at[d, pl.ds(first, count)]
            remote(region, region, rs_s.at[k, d], rs_r.at[k, d], y, me).wait_recv()

        @pl.loop(first, first + count)
        def _(q):
            for half in range(2):
                v = (partial[q, half, mine, :] + sums[0, q, half]) + (sums[1, q, half] + sums[2, q, half])
                if half:
                    both[0][y, q] = v[0:8]
                    both[1][y, q] = v[8:16]
                else:
                    take[q] = v

    sends = []

    def start(cp):
        cp.start()
        sends.append(cp)

    def done(region, s, r):
        remote(region, region, s, r, y, me).wait_recv()

    def rows(p, base=0):
        return pl.ds(base + pl.multiple_of(16 * p, 16), 16)

    for t in range(2):
        for i, step in enumerate((1, -1)):
            start(remote(both[t].at[y], both[t].at[y], b_s.at[t, i], b_r.at[t, i], plane(step), me))

    def slot(s):
        o = s // 2
        second = lax.rem(s, 2)
        early, late = first_pair[o], last_pair[o]
        spot = lax.rem(jnp.maximum(jnp.where(second == 1, late, early), 0), 64)
        return spot, jnp.where(second == 1, late > early, early < 4096).astype(F32)

    @pl.loop(0, 64)
    def _(s):
        spot, filled = slot(s)
        placed1[s] = take[spot] * filled

    def shipment(src, dst, to, s, r):
        return remote(src, dst, s, r, y, to)

    def ship1(dx, d):
        to = peer(dx, d)
        return remote(placed1.at[pl.ds(2 * to, 2)], got.at[pl.ds(2 * me, 2)], a1_s.at[dx, d], a1_r.at[dx, d], y, to)

    def ship2(t, dx, d):
        to = peer(dx, d)
        return remote(placed2.at[to // 8, lax.rem(to, 8), :, pl.ds(32 * t, 32)], out.at[pl.ds(2 * me, 2), pl.ds(64 + 32 * t, 32), :],
                      a2_s.at[t, dx, d], a2_r.at[t, dx, d], y, to)

    def sender(dx, d):
        return index(x - dx, z - d // 2 + 4, lax.rem(c + d, 2))

    def each(dx, f):
        @pl.loop(1 if dx == 0 else 0, 8)
        def _(d):
            f(dx, d)

    order = (0, 1, 3, 2)
    for dx in order:
        each(dx, lambda dx, d: ship1(dx, d).start())
    own1 = pltpu.make_async_copy(placed1.at[pl.ds(2 * me, 2)], got.at[pl.ds(2 * me, 2)], loc.at[4])
    own1.start()
    for t in range(2):
        for i, step in enumerate((1, -1)):
            done(both[t].at[plane(-step)], b_s.at[t, i], b_r.at[t, i])
            region = both[t].at[plane(-step), pl.ds(18 * i, 18)]
            start(remote(region, region, b_s.at[t, 2 + i], b_r.at[t, 2 + i], plane(step), me))
    locals_ = []

    def ship_whole(t):
        for i in range(2):
            done(both[t].at[plane(2), pl.ds(18 * i, 18)], b_s.at[t, 2 + i], b_r.at[t, 2 + i])

        @pl.loop(0, 64)
        def _(s):
            spot, filled = slot(s)
            for p in range(4):
                at = 32 * t + 8 * p
                placed2[s // 16, lax.rem(s // 2, 8), lax.rem(s, 2), at:at + 8, :] = both[t][p, spot] * filled

        for dx in (1, 3, 2, 0):
            each(dx, lambda dx, d: ship2(t, dx, d).start())
        cp = pltpu.make_async_copy(placed2.at[me // 8, lax.rem(me, 8), :, pl.ds(32 * t, 32)],
                                   out.at[pl.ds(2 * me, 2), pl.ds(64 + 32 * t, 32), :], loc.at[5 + t])
        cp.start()
        locals_.append(cp)

    ship_whole(0)
    own1.wait()
    for dx in order:
        each(dx, lambda dx, d: done(got.at[pl.ds(2 * sender(dx, d), 2)], a1_s.at[dx, d], a1_r.at[dx, d]))
        first = 16 * lax.rem(x - dx + 4, 4)
        for i, step in enumerate((1, -1)):
            start(remote(got.at[pl.ds(first, 16)], out.at[pl.ds(first, 16), rows(y), :], w_s.at[dx, i], w_r.at[dx, i], plane(step), me))
        cp = pltpu.make_async_copy(got.at[pl.ds(first, 16)], out.at[pl.ds(first, 16), rows(y), :], loc.at[dx])
        cp.start()
        locals_.append(cp)
    ship_whole(1)
    for dx in order:
        first = 16 * lax.rem(x - dx + 4, 4)
        for i, step in enumerate((1, -1)):
            done(out.at[pl.ds(first, 16), rows(plane(-step)), :], w_s.at[dx, i], w_r.at[dx, i])
            region = out.at[pl.ds(first + 8 * i, 8), rows(plane(-step)), :]
            start(remote(region, region, w_s.at[dx, 2 + i], w_r.at[dx, 2 + i], plane(step), me))
    for dx in order:
        first = 16 * lax.rem(x - dx + 4, 4)
        for i in range(2):
            done(out.at[pl.ds(first + 8 * i, 8), rows(plane(2)), :], w_s.at[dx, 2 + i], w_r.at[dx, 2 + i])
    for t in range(2):
        for dx in order:
            each(dx, lambda dx, d: done(out.at[pl.ds(2 * sender(dx, d), 2), pl.ds(64 + 32 * t, 32), :], a2_s.at[t, dx, d],
                                        a2_r.at[t, dx, d]))
    for cp in locals_:
        cp.wait()
    for cp in rs + sends:
        cp.wait_send()
    for dx in range(4):
        each(dx, lambda dx, d: ship1(dx, d).wait_send())
        for t in range(2):
            each(dx, lambda dx, d: ship2(t, dx, d).wait_send())


def fused(tiles, coeffs, domains, owner, local, aux, first_pair, last_pair):
    vm = pl.BlockSpec(memory_space=pltpu.VMEM)
    sm = pl.BlockSpec(memory_space=pltpu.SMEM)
    hbm = pl.BlockSpec(memory_space=pl.ANY)
    dma = pltpu.SemaphoreType.DMA
    return pl.pallas_call(
        body,
        out_shape=jax.ShapeDtypeStruct((64, 128, 128), F32),
        in_specs=[hbm, hbm, sm, sm, sm, vm, sm, sm],
        out_specs=hbm,
        scratch_shapes=[
            pltpu.VMEM((32, 8, 128, 128), F32), pltpu.VMEM((32, 1024, 256), BF16), pltpu.VMEM((2, 4, 8, 2, 64, 128), F32),
            pltpu.VMEM((1024, 4096), BF16), pltpu.VMEM((1024, 4096), BF16),
            pltpu.VMEM((36, 2, 64, 128), F32), pltpu.VMEM((3, 36, 2, 16, 128), F32), pltpu.VMEM((36, 16, 128), F32),
            pltpu.VMEM((4, 36, 8, 128), F32), pltpu.VMEM((4, 36, 8, 128), F32), pltpu.VMEM((64, 16, 128), F32), pltpu.VMEM((64, 16, 128), F32),
            dma((44,)), dma((44,)), dma((45,)), dma((45,)), dma((6 * len(QUARTERED), 4)), dma((6 * len(QUARTERED), 4)), dma,
            dma((8,)), dma((5, 3)), dma((5, 3)), dma((2, 4)), dma((2, 4)),
            dma((4, 8)), dma((4, 8)), dma((2, 4, 8)), dma((2, 4, 8)), dma((4, 4)), dma((4, 4)), dma((7,))],
        compiler_params=pltpu.CompilerParams(collective_id=1, has_side_effects=True, vmem_limit_bytes=63 * 2**20),
        cost_estimate=pl.CostEstimate(flops=2 * 10**10, bytes_accessed=22 * 10**6, transcendentals=0),
    )(coeffs.reshape(8, 128, 128), tiles.reshape(32, 8, 2, 64, 128), owner, local, aux, domains.reshape(8, 1, 128), first_pair, last_pair)


def copy_body(src, dst, held, into, out_of):
    arrive = [pltpu.make_async_copy(src.at[pl.ds(8 * i, 8)], held.at[pl.ds(8 * i, 8)], into.at[i]) for i in range(8)]
    leave = [pltpu.make_async_copy(held.at[pl.ds(8 * i, 8)], dst.at[pl.ds(8 * i, 8)], out_of.at[i]) for i in range(8)]
    for cp in arrive:
        cp.start()
    for a, b in zip(arrive, leave):
        a.wait()
        b.start()
    for cp in leave:
        cp.wait()


def copied(value):
    hbm = pl.BlockSpec(memory_space=pl.ANY)
    return pl.pallas_call(
        copy_body, in_specs=[hbm], out_specs=hbm, out_shape=jax.ShapeDtypeStruct((64, 128, 128), F32),
        scratch_shapes=[pltpu.VMEM((64, 128, 128), F32), pltpu.SemaphoreType.DMA((8,)), pltpu.SemaphoreType.DMA((8,))],
        compiler_params=pltpu.CompilerParams(vmem_limit_bytes=60 * 2**20))(value)


def on_device(tiles, coeffs, domains, tile_owner, tile_local, tile_aux, pair_owner):
    named = pair_owner[:, 0][None, :] == jnp.arange(32)[:, None]
    code = jnp.asarray(np.arange(36, dtype=np.int32) * 64 + places())[None, :]
    first_pair = jnp.min(jnp.where(named, code, 4096), axis=1)
    last_pair = jnp.max(jnp.where(named, code, -1), axis=1)
    return copied(fused(tiles, coeffs, domains, tile_owner[:, 0], tile_local, tile_aux, first_pair, last_pair))


def solution(mesh):
    placed = (
        P(("grp", "blk"), None, None, None),
        P("blk", None),
        P("blk", None),
        P(("grp", "blk"), None),
        P(("grp", "blk")),
        P(("grp", "blk")),
        P("blk", None),
    )
    return jax.shard_map(
        on_device, mesh=mesh, in_specs=placed, out_specs=P("blk", None, None), check_vma=False
    )
```
